128 devices in a mesh: gx: 16 (over y, x), gy: 8 (over z, core).
Axes of the slice: x: 4, y: 4, z: 4, core: 2. Of those that a mesh axis runs over, the one named last changes fastest.
Arguments:
- features: bfloat16 [64, 64, 64, 128], P('gx', 'gy'), may hold values from -6 to 6
- cell_count: int32 [64, 64], P('gx', 'gy'), may hold values from 32 to 128
- near_mask: int32 [64, 64, 9], P('gx', 'gy'), may hold values 0 or 1
- near_tiles: bfloat16 [64, 64, 9, 128, 128], P('gx', 'gy'), may hold values from -0.1875 to 0.1875
- projection_basis: bfloat16 [64, 64, 32, 128], P('gx', 'gy'), may hold values from -0.5 to 0.5
- expand_basis: bfloat16 [64, 64, 32, 128], P('gx', 'gy'), may hold values from -1 to 1
- far_source: int32 [16, 8, 128], P('gx', 'gy'), may hold values from 0 to 31
- far_owner: int32 [16, 8, 128, 1], P('gx', 'gy'), may hold values from 0 to 127; in each aligned block of 128 rows (0 to 127, 128 to 255, ..., all dimensions but the last counted through in order) at most 2 rows name the same one
- far_cell: int32 [16, 8, 128], P('gx', 'gy'), may hold values from 0 to 31
- distant_pair_matrix: bfloat16 [16, 8, 128, 1024], P('gx', 'gy'), may hold values from -1 to 1
- mixing: bfloat16 [2, 64, 64], replicated, may hold values from -0.75 to 0.75
Outputs:
- result: bfloat16 [64, 64, 64, 128], P('gx', 'gy')
The draws below stay inside these ranges and needn't reach their ends.
Inputs may be any that keep to these rules, and one draw needn't show every extreme that they name: `far_owner`: among the far pairs of one device no owner is named more than 2 times, and one owner is named exactly 2 times on some devices.
All inputs are finite; a program needn't handle non-finite values. No bound on the sum of `near_mask` on one device may be relied on, other than what follows from the above.
Results may differ from the reference program's by a relative error of at most 0.0076.
Values may be sent and summed in bfloat16 or wider, within the bound.
A program may use at most 64 MiB of HBM per device.

```python
import math
import jax
import jax.numpy as jnp
import numpy as np
from jax import lax

C = 64
TILE = 128
RANK = 32
LAYERS = 2
CBX = 4
CBY = 8
NX = 64
NY = 64
CELLS_DEV = 32
PAIRS_DEV = 128
CAP = 2
N_GX = 16
N_GY = 8
DEVICES = 128


def place_ends(values, stream_key, low, top_value):
    shape = values.shape
    spot = [jax.random.randint(jax.random.fold_in(stream_key, axis), (), 0, shape[axis]) for axis in range(len(shape))]
    values = values.at[tuple(spot)].set(low)
    longest = shape.index(max(shape))
    spot[longest] = (spot[longest] + 1) % shape[longest]
    return values.at[tuple(spot)].set(top_value)


def shard_levels(key, shape, split, least, largest):
    gain = 1.0
    for position, blocks in split:
        steps = jax.random.uniform(jax.random.fold_in(jax.random.fold_in(key, 6), position), (blocks,), jnp.float32, least / len(split), largest / len(split))
        gain = gain * jnp.repeat(jnp.exp(steps), shape[position] // blocks).reshape((-1,) + (1,) * (len(shape) - 1 - position))
    return gain


def assign_block(own_key, own, number, rows, number_of, top, most, skew):
    sequence = jax.random.permutation(own_key, number_of)
    crowded, ordinary = load_shares(number_of, rows * top, most, skew, True), load_shares(number_of, rows * top, most, skew, False)
    places = jnp.arange(number_of)

    def named(sizes, turn):
        used = int((sizes > 0).sum())
        fixed = max(1, used // 4)
        shifted = fixed + (places - fixed + turn * (used - fixed)) % max(1, number_of - fixed)
        return jnp.zeros((number_of,), jnp.int32).at[sequence[jnp.where(places < fixed, places, shifted)]].set(jnp.asarray(sizes, jnp.int32))

    sizes = jnp.where(number % 4 == 0, named(crowded, number // 4), named(ordinary, number - number // 4 - 1))
    mixed = jax.random.permutation(jax.random.fold_in(own, 3), number_of)
    source_of, receiver = mixed[0:number_of // 2 * 2:2], mixed[1:number_of // 2 * 2:2]
    slack = jnp.minimum(sizes[source_of] - 1, most - sizes[receiver]) // 2
    slack = jnp.where((source_of == sequence[0]) | (receiver == sequence[0]) | (sizes[receiver] == 0), 0, jnp.maximum(slack, 0))
    shifted = jax.random.randint(jax.random.fold_in(own, 4), (number_of // 2,), 0, 1 << 20) % (slack + 1)
    sizes = sizes.at[source_of].add(-shifted).at[receiver].add(shifted)
    members = jnp.searchsorted(jnp.cumsum(sizes), jnp.arange(rows * top), side="right").astype(jnp.int32)
    table = members.reshape(top, rows).T
    table = table[jax.random.permutation(jax.random.fold_in(own, 1), rows)]
    turn = jax.random.randint(jax.random.fold_in(own, 2), (rows, 1), 0, top)
    return jnp.take_along_axis(table, (jnp.arange(top)[None, :] + turn) % top, axis=1)


def load_shares(count, total, bound, slope, full):
    loads = [(1 << 20) // math.isqrt(standing ** slope) + 1 for standing in range(1, count + 1)]
    largest = bound if full else min(bound, max(-(-total // count), total * loads[0] // sum(loads)))
    least = 1 if total - largest >= count - 1 else 0
    counts, rest = [largest] + [least] * (count - 1), total - largest - least * (count - 1)
    while rest > 0:
        candidates = [i for i in range(1, count) if counts[i] < largest] or [i for i in range(1, count) if counts[i] < bound]
        whole, remaining = sum([loads[i] for i in candidates]), rest
        for i in candidates:
            addition = min(bound - counts[i], max(1, remaining * loads[i] // whole), rest)
            counts[i] = counts[i] + addition
            rest = rest - addition
    return np.array(counts)


def normal_values(own_key, dims, width, bound, pieces=(), kind=jnp.bfloat16):
    gain = shard_levels(own_key, dims, pieces, -0.22, 0.18) if pieces else 1.0
    values = jax.random.normal(own_key, dims, jnp.float32) * width * gain
    return jnp.minimum(jnp.maximum(values, -bound), bound).astype(kind)


def setup_inputs(seed: int = 0) -> dict:
    key_list = jax.random.split(jax.random.key(seed), 12)
    features = normal_values(key_list[0], (NX, NY, C, TILE), 1.0, 6.0, ((0, 16), (1, 8)))
    cell_count = place_ends(jax.random.randint(key_list[1], (NX, NY), TILE // 4, TILE + 1), jax.random.fold_in(key_list[1], 1), TILE // 4, TILE).astype(jnp.int32)
    near_mask = place_ends((jax.random.randint(key_list[2], (NX, NY, 9), 0, 4) < 3).astype(jnp.int32), jax.random.fold_in(key_list[2], 1), 0, 1)
    near_tiles = normal_values(key_list[3], (NX, NY, 9, TILE, TILE), (9 * TILE) ** -0.5, 0.1875, ((0, 16), (1, 8)))
    projection_basis = normal_values(key_list[4], (NX, NY, RANK, TILE), TILE ** -0.5, 0.5, ((0, 16), (1, 8)))
    expand_basis = normal_values(key_list[5], (NX, NY, RANK, TILE), RANK ** -0.5, 1.0, ((0, 16), (1, 8)))
    far_source = place_ends(jax.random.randint(key_list[6], (N_GX, N_GY, PAIRS_DEV), 0, CELLS_DEV), jax.random.fold_in(key_list[6], 1), 0, CELLS_DEV - 1).astype(jnp.int32)
    far_owner_keys = jax.random.split(jax.random.fold_in(key_list[7], 1), N_GX * N_GY * PAIRS_DEV // PAIRS_DEV)
    far_owner_turns = jax.random.permutation(jax.random.fold_in(key_list[7], 3), N_GX * N_GY * PAIRS_DEV // PAIRS_DEV)
    far_owner = jax.vmap(lambda own, number: assign_block(jax.random.fold_in(key_list[7], 2), own, number, PAIRS_DEV, DEVICES, 1, CAP, 2))(far_owner_keys, far_owner_turns).reshape((N_GX, N_GY, PAIRS_DEV, 1))
    far_cell = place_ends(jax.random.randint(key_list[8], (N_GX, N_GY, PAIRS_DEV), 0, CELLS_DEV), jax.random.fold_in(key_list[8], 1), 0, CELLS_DEV - 1).astype(jnp.int32)
    distant_pair_matrix = normal_values(key_list[9], (N_GX, N_GY, PAIRS_DEV, RANK * RANK), RANK ** -0.5, 1.0, ((0, 16), (1, 8)))
    mixing = normal_values(key_list[10], (LAYERS, C, C), C ** -0.5, 0.75)
    return {"features": features, "cell_count": cell_count, "near_mask": near_mask, "near_tiles": near_tiles, "projection_basis": projection_basis, "expand_basis": expand_basis, "far_source": far_source, "far_owner": far_owner, "far_cell": far_cell, "distant_pair_matrix": distant_pair_matrix, "mixing": mixing}


def near_field(x, near_mask, near_tiles):
    def one_row(i):
        tiles_row = lax.dynamic_index_in_dim(near_tiles, i, 0, keepdims=False)
        mask_row = lax.dynamic_index_in_dim(near_mask, i, 0, keepdims=False).astype(jnp.float32)
        total = jnp.zeros((NY, C, TILE), jnp.float32)
        for dx in (-1, 0, 1):
            src_row = lax.dynamic_index_in_dim(x, (i + dx) % NX, 0, keepdims=False)
            for dy in (-1, 0, 1):
                offset = 3 * (dx + 1) + dy + 1
                source = jnp.roll(src_row, -dy, 0).astype(jnp.float32)
                part = jnp.einsum("bcj,bji->bci", source, tiles_row[:, offset].astype(jnp.float32))
                total = total + mask_row[:, offset][:, None, None] * part
        return total
    return lax.map(one_row, jnp.arange(NX, dtype=jnp.int32))


def to_devices(grid):
    shaped = grid.reshape(N_GX, CBX, N_GY, CBY, C, RANK).transpose(0, 2, 1, 3, 4, 5)
    return shaped.reshape(N_GX, N_GY, CELLS_DEV, C, RANK)


def to_grid(local):
    shaped = local.reshape(N_GX, N_GY, CBX, CBY, C, RANK).transpose(0, 2, 1, 3, 4, 5)
    return shaped.reshape(NX, NY, C, RANK)


def reference(features, cell_count, near_mask, near_tiles, projection_basis, expand_basis, far_source, far_owner, far_cell, distant_pair_matrix, mixing):
    live = (jnp.arange(TILE, dtype=jnp.int32)[None, None, :] < cell_count[:, :, None]).astype(jnp.float32)
    x = (features.astype(jnp.float32) * live[:, :, None, :]).astype(jnp.bfloat16)
    pair_linkage = distant_pair_matrix.reshape(N_GX, N_GY, PAIRS_DEV, RANK, RANK).astype(jnp.float32)
    target = (far_owner[..., 0] * CELLS_DEV + far_cell).reshape(-1)
    for layer in range(LAYERS):
        near = near_field(x, near_mask, near_tiles)
        coef = jnp.einsum("abcp,abrp->abcr", x.astype(jnp.float32), projection_basis.astype(jnp.float32)).astype(jnp.bfloat16)
        local_coef = to_devices(coef)
        picked_entries = jnp.take_along_axis(local_coef, far_source[:, :, :, None, None], axis=2)
        term = jnp.einsum("abpcr,abprs->abpcs", picked_entries.astype(jnp.float32), pair_linkage).astype(jnp.bfloat16)
        summed = jnp.zeros((DEVICES * CELLS_DEV, C, RANK), jnp.float32)
        summed = summed.at[target].add(term.reshape(-1, C, RANK).astype(jnp.float32))
        gathered = to_grid(summed).astype(jnp.bfloat16)
        far = jnp.einsum("abcr,abrp->abcp", gathered.astype(jnp.float32), expand_basis.astype(jnp.float32))
        mixed = jnp.einsum("dc,abcp->abdp", mixing[layer].astype(jnp.float32), x.astype(jnp.float32))
        hidden = mixed + near + far
        x = (jax.nn.gelu(hidden, approximate=False) * live[:, :, None, :]).astype(jnp.bfloat16)
    return x
```

```python
import functools

import jax
import jax.numpy as jnp
from jax import lax
from jax.experimental import pallas as pl
from jax.experimental.pallas import tpu as pltpu
from jax.sharding import PartitionSpec as P

LAYERS = 2
MESH = pl.DeviceIdType.MESH


def exchange_kernel(wide_x, wide_y, box_ref, got_ref, inbox, send_sem, recv_sem, row_sem):
    a, b = lax.axis_index("gx"), lax.axis_index("gy")
    me = a * wide_y + b
    count = wide_x * wide_y

    def along_x(step):
        return lax.rem(a + step, wide_x), b

    def along_y(step):
        return a, lax.rem(b + step, wide_y)

    barrier = pltpu.get_barrier_semaphore()
    for step in range(1, wide_y):
        pl.semaphore_signal(barrier, inc=1, device_id=along_y(step), device_id_type=MESH)
    for step in range(1, wide_x):
        pl.semaphore_signal(barrier, inc=1, device_id=along_x(step), device_id_type=MESH)
    pl.semaphore_wait(barrier, wide_x + wide_y - 2)
    for step in range(1, wide_x):
        pl.semaphore_signal(row_sem, inc=1, device_id=along_x(step), device_id_type=MESH)
    pl.semaphore_wait(row_sem, wide_x - 1)

    def send(step, carry):
        other = lax.rem(me + step, count)
        pltpu.make_async_remote_copy(
            src_ref=box_ref.at[other],
            dst_ref=inbox.at[me],
            send_sem=send_sem,
            recv_sem=recv_sem,
            device_id=(other // wide_y, lax.rem(other, wide_y)),
            device_id_type=MESH,
        ).start()
        return carry

    lax.fori_loop(1, count, send, 0)
    own = pltpu.make_async_copy(box_ref.at[me], inbox.at[me], recv_sem)
    own.start()
    pltpu.make_async_copy(box_ref, inbox, recv_sem).wait()
    rest = pl.ds(0, count - 1)
    pltpu.make_async_copy(box_ref.at[rest], inbox.at[rest], send_sem).wait()
    got_ref[...] = inbox[...]


def exchange(box):
    wide_x, wide_y = lax.axis_size("gx"), lax.axis_size("gy")
    return pl.pallas_call(
        functools.partial(exchange_kernel, wide_x, wide_y),
        out_shape=jax.ShapeDtypeStruct(box.shape, box.dtype),
        in_specs=[pl.BlockSpec(memory_space=pltpu.VMEM)],
        out_specs=pl.BlockSpec(memory_space=pltpu.VMEM),
        scratch_shapes=[
            pltpu.VMEM(box.shape, box.dtype),
            pltpu.SemaphoreType.DMA,
            pltpu.SemaphoreType.DMA,
            pltpu.SemaphoreType.REGULAR,
        ],
        compiler_params=pltpu.CompilerParams(
            collective_id=0, has_side_effects=True, vmem_limit_bytes=32 << 20
        ),
    )(box)


def extended(cells, sides, width):
    for axis, dim in sides:
        count = lax.axis_size(axis)
        head = lax.slice_in_dim(cells, 0, width, axis=dim)
        tail = lax.slice_in_dim(cells, cells.shape[dim] - width, cells.shape[dim], axis=dim)
        cells = jnp.concatenate(
            [
                lax.ppermute(tail, axis, [(i, (i + 1) % count) for i in range(count)]),
                cells,
                lax.ppermute(head, axis, [((i + 1) % count, i) for i in range(count)]),
            ],
            axis=dim,
        )
    return cells


def shards(
    features,
    cell_count,
    near_mask,
    near_tiles,
    projection_basis,
    expand_basis,
    far_source,
    far_owner,
    far_cell,
    distant_pair_matrix,
    mixing,
):
    cells_x, cells_y, chans, slots = features.shape
    rank = projection_basis.shape[2]
    cells = cells_x * cells_y
    pairs = far_source.shape[2]
    wide_x = lax.axis_size("gx")
    wide_y = lax.axis_size("gy")
    device_list = wide_x * wide_y
    capacity = max(2, 2 * pairs // device_list)
    live = (jnp.arange(slots, dtype=jnp.int32)[None, None, :] < cell_count[:, :, None]).astype(
        jnp.float32
    )
    x = (features.astype(jnp.float32) * live[:, :, None, :]).astype(jnp.bfloat16)
    owner = far_owner[0, 0, :, 0]
    source = far_source[0, 0]
    target_cell = far_cell[0, 0]
    pair_linkage = distant_pair_matrix[0, 0].reshape(pairs, rank, rank)
    onehot = (owner[:, None] == jnp.arange(device_list, dtype=jnp.int32)[None, :]).astype(jnp.int32)
    previous_state = jnp.cumsum(onehot, axis=0) - onehot
    position = owner * capacity + jnp.sum(previous_state * onehot, axis=1)
    weights_mask = near_mask.astype(jnp.float32)
    for layer in range(LAYERS):
        padded = extended(x, (("gx", 0), ("gy", 1)), 1)
        near = jnp.zeros((cells_x, cells_y, chans, slots), jnp.float32)
        for dx in (-1, 0, 1):
            for dy in (-1, 0, 1):
                offset = 3 * (dx + 1) + dy + 1
                shifted = padded[1 + dx : 1 + dx + cells_x, 1 + dy : 1 + dy + cells_y]
                part = jnp.einsum(
                    "abcj,abji->abci",
                    shifted,
                    near_tiles[:, :, offset],
                    preferred_element_type=jnp.float32,
                )
                near = near + weights_mask[:, :, offset][:, :, None, None] * part
        coef = jnp.einsum(
            "abcp,abrp->abcr", x, projection_basis, preferred_element_type=jnp.float32
        ).astype(jnp.bfloat16)
        picked_entries = coef.reshape(cells, chans, rank)[source]
        term = jnp.einsum(
            "nik,nku->niu", picked_entries, pair_linkage, preferred_element_type=jnp.float32
        ).astype(jnp.bfloat16)
        outbox = (
            jnp.zeros((device_list * capacity, chans * rank), jnp.bfloat16)
            .at[position]
            .set(term.reshape(pairs, chans * rank))
        )
        labels = jnp.zeros((device_list * capacity,), jnp.int32).at[position].set(target_cell)
        inbox = exchange(outbox.reshape(device_list, capacity * chans * rank // 128, 128))
        inbox = inbox.reshape(device_list * capacity, chans * rank)
        incoming_labels = lax.all_to_all(
            labels, ("gx", "gy"), split_axis=0, concat_axis=0, tiled=True
        )
        selection_mask = (
            incoming_labels[:, None] == jnp.arange(cells, dtype=jnp.int32)[None, :]
        ).astype(jnp.bfloat16)
        summed = jnp.einsum("sk,sf->kf", selection_mask, inbox, preferred_element_type=jnp.float32)
        gathered = summed.astype(jnp.bfloat16).reshape(cells_x, cells_y, chans, rank)
        far = jnp.einsum(
            "abcr,abrp->abcp", gathered, expand_basis, preferred_element_type=jnp.float32
        )
        mixed = jnp.einsum("dc,abcp->abdp", mixing[layer], x, preferred_element_type=jnp.float32)
        hidden = mixed + near + far
        x = (jax.nn.gelu(hidden, approximate=False) * live[:, :, None, :]).astype(jnp.bfloat16)
    return x


def solution(mesh):
    placed = (
        P("gx", "gy", None, None),
        P("gx", "gy"),
        P("gx", "gy", None),
        P("gx", "gy", None, None, None),
        P("gx", "gy", None, None),
        P("gx", "gy", None, None),
        P("gx", "gy", None),
        P("gx", "gy", None, None),
        P("gx", "gy", None),
        P("gx", "gy", None, None),
        P(),
    )
    return jax.shard_map(
        shards, mesh=mesh, in_specs=placed, out_specs=P("gx", "gy", None, None), check_vma=False
    )
```

```python
import functools

import jax
import jax.numpy as jnp
from jax import lax
from jax.experimental import pallas as pl
from jax.experimental.pallas import tpu as pltpu
from jax.sharding import PartitionSpec as P

LAYERS = 2
HALVES = 2
OFFSETS = 9
MESH = pl.DeviceIdType.MESH
BF = jnp.bfloat16
F32 = jnp.float32
ROWS = 16
LANES = 128
RANK = 32


def iota(shape, dim):
    return lax.broadcasted_iota(jnp.int32, shape, dim)


def one(condition, kind=F32):
    return jnp.where(condition, 1.0, 0.0).astype(kind)


def dot(a, b):
    return jnp.dot(a, b, preferred_element_type=F32)


def dot_t(a, b):
    return lax.dot_general(a, b, (((1,), (1,)), ((), ())), preferred_element_type=F32)


def gelu(v):
    return 0.5 * v * (1.0 + lax.erf(v * 0.7071067811865476))


def kernel(
    wide_x,
    wide_y,
    cells_x,
    cells_y,
    count_ref,
    mask_ref,
    feat_ref,
    tiles_hbm,
    proj_ref,
    exp_ref,
    src_ref,
    own_ref,
    cell_ref,
    pair_ref,
    mix_ref,
    res_ref,
    tiles,
    wt,
    xe,
    basis,
    out,
    inbox,
    flat,
    sums,
    exp4,
    lab_out,
    lab_in,
    sel,
    idx,
    idx_s,
    near,
    live,
    tile_sem,
    idx_sem,
    send_sem,
    recv_sem,
    halo_send,
    halo_recv,
    lab_sem,
    row_sem,
):
    a, b = lax.axis_index("gx"), lax.axis_index("gy")
    count = wide_x * wide_y
    me = a * wide_y + b
    cells = cells_x * cells_y
    half = 2 * ROWS

    def peer(da, db):
        return lax.rem(a + da + wide_x, wide_x), lax.rem(b + db + wide_y, wide_y)

    def signal(sem, where):
        pl.semaphore_signal(sem, inc=1, device_id=where, device_id_type=MESH)

    barrier = pltpu.get_barrier_semaphore()
    for step in range(1, wide_y):
        signal(barrier, peer(0, step))
    for step in range(1, wide_x):
        signal(barrier, peer(step, 0))
    for da in (-1, 1):
        for db in (-1, 1):
            signal(barrier, peer(da, db))

    parts = tile_sem.shape[0]
    size = cells * OFFSETS // parts

    def tile_copy(n):
        rows = pl.ds(n * size, size)
        return pltpu.make_async_copy(tiles_hbm.at[rows], tiles.at[rows], tile_sem.at[n])

    for n in range(parts):
        tile_copy(n).start()

    lane = iota((1, LANES), 1)
    slot_of = (lane // RANK) % 2
    first_slot = slot_of == 0
    first_ch = lane < 2 * RANK

    for c in range(cells):
        i, j = c // cells_y, c % cells_y
        alive = one(lane < count_ref[i, j])
        live[pl.ds(c, 1), :] = alive
        xe[0, i + 1, j + 1] = (feat_ref[c].astype(F32) * alive).astype(BF)

    owner = own_ref[0]
    named = one(iota((count, LANES), 0) == owner)
    before = dot(named.astype(BF), one(iota((LANES, LANES), 0) < iota((LANES, LANES), 1), BF))
    slot0 = jnp.where(before < 0.5, named, 0.0)
    slots = (slot0.astype(BF), (named - slot0).astype(BF))
    source = jnp.broadcast_to(src_ref[0], (8, LANES)).astype(F32).astype(BF)
    target = cell_ref[0]
    labels = jnp.zeros((count, LANES), F32)
    for k in range(2):
        idx[k] = dot_t(source, slots[k]).astype(jnp.int32)
        wanted = one(iota((LANES, LANES), 0) == target + k * cells, BF)
        labels = labels + dot_t(slots[k], wanted)
    lab_out[...] = labels
    to_scalars = pltpu.make_async_copy(idx, idx_s, idx_sem)
    to_scalars.start()

    for k in range(2):
        for j in range(RANK * RANK // LANES):
            flat[pl.ds(k * 8 + j, count, stride=ROWS), :] = dot(
                slots[k], pair_ref[:, j * LANES : (j + 1) * LANES]
            )
    fold_row, fold_col = iota((2 * LANES, LANES), 0), iota((2 * LANES, LANES), 1)
    fold = one(
        (fold_row % RANK == fold_col % RANK) & (fold_row // LANES == (fold_col // RANK) % 2), BF
    )
    quarter = [one(lane // RANK == q) for q in range(4)]
    block = 8

    def place(n, carry):
        lhs = []
        for d in range(block):
            v = flat[pl.ds((n * block + d) * ROWS, ROWS), :]
            lhs.append(
                jnp.concatenate(
                    [
                        jnp.concatenate([v[k * 8 : k * 8 + 8] * q for q in quarter], axis=0)
                        for k in range(2)
                    ],
                    axis=1,
                )
            )
        got = dot(jnp.concatenate(lhs, axis=0).astype(BF), fold)
        for d in range(block):
            r = got[d * RANK : (d + 1) * RANK]
            for q in range(4):
                wt[n * block + d, q * RANK : (q + 1) * RANK, :] = (r * quarter[q]).astype(BF)
        return carry

    lax.fori_loop(0, count // block, place, 0)

    spread_row, spread_col = iota((RANK, LANES), 0), iota((RANK, LANES), 1) % RANK
    spread = one(spread_row == 4 * (spread_col % 8) + spread_col // 8, BF)

    def project(layer, halves):
        lo, rows = halves[0] * half, len(halves) * half

        def body(c, carry):
            x = xe[layer, c // cells_y + 1, lax.rem(c, cells_y) + 1, lo : lo + rows, :]
            coef = dot_t(x, proj_ref[c]).astype(BF)
            wide = dot(coef, spread)
            for n, h in enumerate(halves):
                top = wide[n * half : n * half + ROWS]
                low = wide[n * half + ROWS : (n + 1) * half]
                basis[h, c] = jnp.where(first_ch, top, low).astype(BF)
            return carry

        lax.fori_loop(0, cells, body, 0, unroll=4)

    project(0, (0, 1))
    for c in range(cells):
        exp4[c] = jnp.concatenate([exp_ref[c]] * 4, axis=0)

    links = [
        (1, 0, (cells_x, pl.ds(1, cells_y)), (0, pl.ds(1, cells_y))),
        (-1, 0, (1, pl.ds(1, cells_y)), (cells_x + 1, pl.ds(1, cells_y))),
        (0, 1, (pl.ds(1, cells_x), cells_y), (pl.ds(1, cells_x), 0)),
        (0, -1, (pl.ds(1, cells_x), 1), (pl.ds(1, cells_x), cells_y + 1)),
        (1, 1, (cells_x, cells_y), (0, 0)),
        (1, -1, (cells_x, 1), (0, cells_y + 1)),
        (-1, 1, (1, cells_y), (cells_x + 1, 0)),
        (-1, -1, (1, 1), (cells_x + 1, cells_y + 1)),
    ]

    def halo(layer, part, rows, n):
        da, db, (si, sj), (ti, tj) = links[n]
        return pltpu.make_async_remote_copy(
            src_ref=xe.at[layer, si, sj, rows],
            dst_ref=xe.at[layer, ti, tj, rows],
            send_sem=halo_send.at[part, n],
            recv_sem=halo_recv.at[part, n],
            device_id=peer(da, db),
            device_id_type=MESH,
        )

    everything = pl.ds(0, 2 * half)
    halo_parts = [(0, everything), (1, pl.ds(0, half)), (1, pl.ds(half, half))]

    def halo_start(part):
        layer, rows = halo_parts[part]
        for n in range(len(links)):
            halo(layer, part, rows, n).start()

    def halo_wait(part):
        layer, rows = halo_parts[part]
        for n in range(len(links)):
            halo(layer, part, rows, n).wait_recv()

    pl.semaphore_wait(barrier, wide_x + wide_y - 2 + 4)
    for step in range(1, wide_x):
        signal(row_sem, peer(step, 0))
    halo_start(0)
    to_scalars.wait()

    def other_of(step):
        return lax.rem(me + 1 + step, count)

    def terms(rounds, halves):
        def body(n, carry):
            for d in range(block):
                o = other_of(n * block + d)
                s0, s1 = [lax.clamp(0, idx_s[k, 0, o], cells - 1) for k in range(2)]
                lhs = jnp.concatenate(
                    [jnp.where(first_slot, basis[h, s0], basis[h, s1]) for h in halves], axis=0
                )
                got = dot(lhs, wt[o]).astype(BF)
                for m, r in enumerate(rounds):
                    out[r, o] = got[m * ROWS : (m + 1) * ROWS]
            return carry

        lax.fori_loop(0, count // block, body, 0)

    def send(r):
        def body(step, carry):
            o = other_of(step)
            pltpu.make_async_remote_copy(
                src_ref=out.at[r, o],
                dst_ref=inbox.at[r, me],
                send_sem=send_sem.at[r],
                recv_sem=recv_sem.at[r],
                device_id=(o // wide_y, lax.rem(o, wide_y)),
                device_id_type=MESH,
            ).start()
            return carry

        lax.fori_loop(0, count - 1, body, 0)
        pltpu.make_async_copy(out.at[r, me], inbox.at[r, me], recv_sem.at[r]).start()

    def send_labels():
        def body(step, carry):
            o = other_of(step)
            pltpu.make_async_remote_copy(
                src_ref=lab_out.at[pl.ds(o, 1)],
                dst_ref=lab_in.at[pl.ds(me, 1)],
                send_sem=lab_sem.at[0],
                recv_sem=lab_sem.at[1],
                device_id=(o // wide_y, lax.rem(o, wide_y)),
                device_id_type=MESH,
            ).start()
            return carry

        lax.fori_loop(0, count - 1, body, 0)
        pltpu.make_async_copy(
            lab_out.at[pl.ds(me, 1)], lab_in.at[pl.ds(me, 1)], lab_sem.at[1]
        ).start()

    def receive(r):
        pltpu.make_async_copy(out.at[r], inbox.at[r], recv_sem.at[r]).wait()

    def near_field(layer):
        mix = mix_ref[layer]

        def body(c, carry):
            i, j = c // cells_y, lax.rem(c, cells_y)
            lhs = []
            for o in range(OFFSETS):
                active = mask_ref[i, j, o].astype(F32).astype(BF)
                lhs.append(xe[layer, i + o // 3, j + o % 3] * active)
            weights = tiles[pl.ds(c * OFFSETS, OFFSETS)].reshape(OFFSETS * LANES, LANES)
            near[c] = dot(jnp.concatenate(lhs, axis=1), weights) + dot(
                mix, xe[layer, i + 1, j + 1]
            )
            return carry

        lax.fori_loop(0, cells, body, 0)

    def gather(r):
        flat[: count * ROWS, :] = inbox[r].reshape(count * ROWS, LANES).astype(F32)
        chosen = sel[...]
        for row in range(ROWS):
            v = flat[pl.ds(row, count, stride=ROWS), :].astype(BF)
            got = dot(chosen, v)
            sums[pl.ds(row, cells, stride=ROWS), :] = got[:cells] + pltpu.roll(
                got[cells : 2 * cells], LANES - RANK, 1
            )

    def finish(layer, h):
        def body(c, carry):
            g = sums[pl.ds(c * ROWS, ROWS), :]
            lhs = jnp.concatenate(
                [jnp.where(first_slot & first_ch, g, 0.0), jnp.where(first_slot & ~first_ch, g, 0.0)],
                axis=0,
            ).astype(BF)
            hidden = near[c, h * half : (h + 1) * half, :] + dot(lhs, exp4[c])
            x = (gelu(hidden) * live[pl.ds(c, 1), :]).astype(BF)
            if layer + 1 < LAYERS:
                xe[layer + 1, c // cells_y + 1, lax.rem(c, cells_y) + 1, h * half : (h + 1) * half, :] = x
            else:
                res_ref[c, h * half : (h + 1) * half, :] = x
            return carry

        lax.fori_loop(0, cells, body, 0, unroll=2)

    terms((0, 1), (0, 1))
    pl.semaphore_wait(row_sem, wide_x - 1)
    send_labels()
    send(0)
    send(1)
    for n in range(parts):
        tile_copy(n).wait()
    halo_wait(0)
    near_field(0)
    pltpu.make_async_copy(lab_out, lab_in, lab_sem.at[1]).wait()
    sel[...] = jnp.transpose(lab_in[...])[: 2 * cells].astype(BF)
    for h in range(HALVES):
        receive(h)
        gather(h)
        finish(0, h)
        halo_start(1 + h)
        project(1, (h,))
        terms((2 + h,), (h,))
        send(2 + h)
    halo_wait(1)
    halo_wait(2)
    near_field(1)
    for h in range(HALVES):
        receive(2 + h)
        gather(2 + h)
        finish(1, h)

    rest = pl.ds(0, count - 1)
    for r in range(2 * LAYERS):
        pltpu.make_async_copy(out.at[r, rest], inbox.at[r, rest], send_sem.at[r]).wait()
    pltpu.make_async_copy(lab_out.at[rest], lab_in.at[rest], lab_sem.at[0]).wait()
    for part, (layer, rows) in enumerate(halo_parts):
        for n in range(len(links)):
            halo(layer, part, rows, n).wait_send()


def shards(
    features,
    cell_count,
    near_mask,
    near_tiles,
    projection_basis,
    expand_basis,
    far_source,
    far_owner,
    far_cell,
    distant_pair_matrix,
    mixing,
):
    cells_x, cells_y, chans, slots = features.shape
    rank = projection_basis.shape[2]
    cells = cells_x * cells_y
    pairs = far_source.shape[2]
    wide_x, wide_y = lax.axis_size("gx"), lax.axis_size("gy")
    count = wide_x * wide_y
    vmem = pl.BlockSpec(memory_space=pltpu.VMEM)
    smem = pl.BlockSpec(memory_space=pltpu.SMEM)
    hbm = pl.BlockSpec(memory_space=pl.ANY)
    rounds = 2 * LAYERS
    result = pl.pallas_call(
        functools.partial(kernel, wide_x, wide_y, cells_x, cells_y),
        out_shape=jax.ShapeDtypeStruct((cells, chans, slots), BF),
        in_specs=[smem, smem, vmem, hbm] + [vmem] * 7,
        out_specs=vmem,
        scratch_shapes=[
            pltpu.VMEM((cells * OFFSETS, slots, slots), BF),
            pltpu.VMEM((count, LANES, LANES), BF),
            pltpu.VMEM((LAYERS, cells_x + 2, cells_y + 2, chans, slots), BF),
            pltpu.VMEM((HALVES, cells, ROWS, LANES), BF),
            pltpu.VMEM((rounds, count, ROWS, LANES), BF),
            pltpu.VMEM((rounds, count, ROWS, LANES), BF),
            pltpu.VMEM((count * ROWS + ROWS, LANES), F32),
            pltpu.VMEM((cells * ROWS + ROWS, LANES), F32),
            pltpu.VMEM((cells, 4 * rank, slots), BF),
            pltpu.VMEM((count, LANES), F32),
            pltpu.VMEM((count, LANES), F32),
            pltpu.VMEM((2 * cells, count), BF),
            pltpu.VMEM((2, 8, LANES), jnp.int32),
            pltpu.SMEM((2, 8, LANES), jnp.int32),
            pltpu.VMEM((cells, chans, slots), F32),
            pltpu.VMEM((cells, slots), F32),
            pltpu.SemaphoreType.DMA((4,)),
            pltpu.SemaphoreType.DMA,
            pltpu.SemaphoreType.DMA((rounds,)),
            pltpu.SemaphoreType.DMA((rounds,)),
            pltpu.SemaphoreType.DMA((3, 8)),
            pltpu.SemaphoreType.DMA((3, 8)),
            pltpu.SemaphoreType.DMA((2,)),
            pltpu.SemaphoreType.REGULAR,
        ],
        compiler_params=pltpu.CompilerParams(
            collective_id=0, has_side_effects=True, vmem_limit_bytes=48 << 20
        ),
    )(
        cell_count,
        near_mask,
        features.reshape(cells, chans, slots),
        near_tiles.reshape(cells * OFFSETS, slots, slots),
        projection_basis.reshape(cells, rank, slots),
        expand_basis.reshape(cells, rank, slots),
        far_source.reshape(1, pairs),
        far_owner.reshape(1, pairs),
        far_cell.reshape(1, pairs),
        distant_pair_matrix.reshape(pairs, rank * rank),
        mixing,
    )
    return result.reshape(cells_x, cells_y, chans, slots)


def solution(mesh):
    placed = (
        P("gx", "gy", None, None),
        P("gx", "gy"),
        P("gx", "gy", None),
        P("gx", "gy", None, None, None),
        P("gx", "gy", None, None),
        P("gx", "gy", None, None),
        P("gx", "gy", None),
        P("gx", "gy", None, None),
        P("gx", "gy", None),
        P("gx", "gy", None, None),
        P(),
    )
    return jax.shard_map(
        shards, mesh=mesh, in_specs=placed, out_specs=P("gx", "gy", None, None), check_vma=False
    )
```

```python
import functools

import jax
import jax.numpy as jnp
from jax import lax
from jax.experimental import pallas as pl
from jax.experimental.pallas import tpu as pltpu
from jax.sharding import PartitionSpec as P

LAYERS = 2
HALVES = 2
OFFSETS = 9
MESH = pl.DeviceIdType.MESH
BF = jnp.bfloat16
F32 = jnp.float32
ROWS = 16
LANES = 128
RANK = 32


def iota(shape, dim):
    return lax.broadcasted_iota(jnp.int32, shape, dim)


def one(condition, kind=F32):
    return jnp.where(condition, 1.0, 0.0).astype(kind)


def dot(a, b):
    return jnp.dot(a, b, preferred_element_type=F32)


def dot_t(a, b):
    return lax.dot_general(a, b, (((1,), (1,)), ((), ())), preferred_element_type=F32)


def gelu(v):
    return 0.5 * v * (1.0 + lax.erf(v * 0.7071067811865476))


def kernel(
    wide_x,
    wide_y,
    cells_x,
    cells_y,
    count_hbm,
    mask_hbm,
    feat_hbm,
    tiles_hbm,
    proj_hbm,
    exp_hbm,
    src_hbm,
    own_hbm,
    cell_hbm,
    pair_hbm,
    mix_hbm,
    res_ref,
    count_ref,
    mask_ref,
    feat_ref,
    proj_ref,
    exp_ref,
    src_ref,
    own_ref,
    cell_ref,
    pair_ref,
    mix_ref,
    proj4,
    load_sem,
    tiles,
    wt,
    xe,
    basis,
    out,
    inbox,
    flat,
    sums,
    exp4,
    lab_out,
    lab_mid,
    lab_turn,
    lab_in,
    sel,
    idx,
    idx_s,
    near,
    live,
    tile_sem,
    idx_sem,
    send_sem,
    recv_sem,
    halo_send,
    halo_recv,
    lab_sem,
    row_sem,
):
    a, b = lax.axis_index("gx"), lax.axis_index("gy")
    count = wide_x * wide_y
    me = a * wide_y + b
    cells = cells_x * cells_y
    half = 2 * ROWS

    def peer(da, db):
        return lax.rem(a + da + wide_x, wide_x), lax.rem(b + db + wide_y, wide_y)

    def signal(sem, where):
        pl.semaphore_signal(sem, inc=1, device_id=where, device_id_type=MESH)

    loads = [
        pltpu.make_async_copy(hbm, ref, load_sem.at[n])
        for n, (hbm, ref) in enumerate(
            [
                (count_hbm, count_ref),
                (feat_hbm, feat_ref),
                (src_hbm, src_ref),
                (own_hbm, own_ref),
                (cell_hbm, cell_ref),
                (pair_hbm, pair_ref),
                (proj_hbm, proj_ref),
                (exp_hbm, exp_ref),
                (mask_hbm, mask_ref),
                (mix_hbm, mix_ref),
            ]
        )
    ]
    for load in loads:
        load.start()

    barrier = pltpu.get_barrier_semaphore()
    for step in range(1, wide_y):
        signal(barrier, peer(0, step))
    for step in range(1, wide_x):
        signal(barrier, peer(step, 0))
    for da in (-1, 1):
        for db in (-1, 1):
            signal(barrier, peer(da, db))

    parts = tile_sem.shape[0]
    size = cells * OFFSETS // parts

    def tile_copy(n):
        rows = pl.ds(n * size, size)
        return pltpu.make_async_copy(tiles_hbm.at[rows], tiles.at[rows], tile_sem.at[n])

    for n in range(parts):
        tile_copy(n).start()

    lane = iota((1, LANES), 1)
    slot_of = (lane // RANK) % 2
    first_slot = slot_of == 0
    first_ch = lane < 2 * RANK

    for load in loads[:2]:
        load.wait()

    def enter(c, carry):
        i, j = c // cells_y, lax.rem(c, cells_y)
        alive = one(lane < count_ref[i, j])
        live[pl.ds(c, 1), :] = alive
        xe[0, i + 1, j + 1] = (feat_ref[c].astype(F32) * alive).astype(BF)
        return carry

    with jax.named_scope("enter"):
        lax.fori_loop(0, cells, enter, 0, unroll=4)

    for load in loads[2:]:
        load.wait()
    owner = own_ref[0]
    named = one(iota((count, LANES), 0) == owner)
    before = dot(named.astype(BF), one(iota((LANES, LANES), 0) < iota((LANES, LANES), 1), BF))
    slot0 = jnp.where(before < 0.5, named, 0.0)
    slots = (slot0.astype(BF), (named - slot0).astype(BF))
    source = jnp.broadcast_to(src_ref[0], (8, LANES)).astype(F32).astype(BF)
    target = cell_ref[0]
    labels = jnp.zeros((count, LANES), F32)
    for k in range(2):
        idx[k] = dot_t(source, slots[k]).astype(jnp.int32)
        wanted = one(iota((LANES, LANES), 0) == target + k * cells, BF)
        labels = labels + dot_t(slots[k], wanted)
    by_row, by_col = iota((count, LANES), 0), iota((count, LANES), 1)
    by_column = one(by_col == by_row % wide_x * wide_y + by_row // wide_x, BF)
    lab_out[...] = dot(by_column, labels.astype(BF))
    to_scalars = pltpu.make_async_copy(idx, idx_s, idx_sem)
    to_scalars.start()

    for k in range(2):
        for j in range(RANK * RANK // LANES):
            flat[pl.ds(k * 8 + j, count, stride=ROWS), :] = dot(
                slots[k], pair_ref[:, j * LANES : (j + 1) * LANES]
            )
    fold_row, fold_col = iota((2 * LANES, LANES), 0), iota((2 * LANES, LANES), 1)
    fold = one(
        (fold_row % RANK == fold_col % RANK) & (fold_row // LANES == (fold_col // RANK) % 2), BF
    )
    quarter = [one(lane // RANK == q) for q in range(4)]
    quarter_bf = [q.astype(BF) for q in quarter]
    block = 8

    def place(n, carry):
        lhs = []
        for d in range(block):
            v = flat[pl.ds((n * block + d) * ROWS, ROWS), :]
            lhs.append(
                jnp.concatenate(
                    [
                        jnp.concatenate([v[k * 8 : k * 8 + 8] * q for q in quarter], axis=0)
                        for k in range(2)
                    ],
                    axis=1,
                )
            )
        got = dot(jnp.concatenate(lhs, axis=0).astype(BF), fold).astype(BF)
        for d in range(block):
            r = got[d * RANK : (d + 1) * RANK]
            for q in range(4):
                wt[n * block + d, q * RANK : (q + 1) * RANK, :] = r * quarter_bf[q]
        return carry

    with jax.named_scope("place"):
        lax.fori_loop(0, count // block, place, 0, unroll=2)

    links = [
        (1, 0, (cells_x, pl.ds(1, cells_y)), (0, pl.ds(1, cells_y))),
        (-1, 0, (1, pl.ds(1, cells_y)), (cells_x + 1, pl.ds(1, cells_y))),
        (0, 1, (pl.ds(1, cells_x), cells_y), (pl.ds(1, cells_x), 0)),
        (0, -1, (pl.ds(1, cells_x), 1), (pl.ds(1, cells_x), cells_y + 1)),
        (1, 1, (cells_x, cells_y), (0, 0)),
        (1, -1, (cells_x, 1), (0, cells_y + 1)),
        (-1, 1, (1, cells_y), (cells_x + 1, 0)),
        (-1, -1, (1, 1), (cells_x + 1, cells_y + 1)),
    ]

    def halo(layer, part, rows, n):
        da, db, (si, sj), (ti, tj) = links[n]
        return pltpu.make_async_remote_copy(
            src_ref=xe.at[layer, si, sj, rows],
            dst_ref=xe.at[layer, ti, tj, rows],
            send_sem=halo_send.at[part, n],
            recv_sem=halo_recv.at[part, n],
            device_id=peer(da, db),
            device_id_type=MESH,
        )

    everything = pl.ds(0, 2 * half)
    halo_parts = [(0, everything), (1, pl.ds(0, half)), (1, pl.ds(half, half))]

    def halo_start(part):
        layer, rows = halo_parts[part]
        for n in range(len(links)):
            halo(layer, part, rows, n).start()

    def halo_wait(part):
        layer, rows = halo_parts[part]
        for n in range(len(links)):
            halo(layer, part, rows, n).wait_recv()

    def labels_along_y():
        for step in range(1, wide_y):
            there = peer(0, step)
            pltpu.make_async_remote_copy(
                src_ref=lab_out.at[pl.ds(pl.multiple_of(there[1] * wide_x, wide_x), wide_x)],
                dst_ref=lab_mid.at[pl.ds(pl.multiple_of(b * wide_x, wide_x), wide_x)],
                send_sem=lab_sem.at[0],
                recv_sem=lab_sem.at[1],
                device_id=there,
                device_id_type=MESH,
            ).start()
        mine = pl.ds(pl.multiple_of(b * wide_x, wide_x), wide_x)
        lab_mid[mine, :] = lab_out[mine, :]

    def labels_along_x():
        some = pl.ds(0, count - wide_x)
        pltpu.make_async_copy(lab_out.at[some], lab_mid.at[some], lab_sem.at[1]).wait()
        lab_turn[...] = lax.dot_general(
            by_column,
            lab_mid[...].astype(BF),
            (((0,), (0,)), ((), ())),
            preferred_element_type=F32,
        )
        for step in range(1, wide_x):
            there = peer(step, 0)
            pltpu.make_async_remote_copy(
                src_ref=lab_turn.at[pl.ds(pl.multiple_of(there[0] * wide_y, wide_y), wide_y)],
                dst_ref=lab_in.at[pl.ds(pl.multiple_of(a * wide_y, wide_y), wide_y)],
                send_sem=lab_sem.at[2],
                recv_sem=lab_sem.at[3],
                device_id=there,
                device_id_type=MESH,
            ).start()
        mine = pl.ds(pl.multiple_of(a * wide_y, wide_y), wide_y)
        lab_in[mine, :] = lab_turn[mine, :]

    with jax.named_scope("barrier_near"):
        pl.semaphore_wait(barrier, wide_x + wide_y - 2 + 4)
    for step in range(1, wide_x):
        signal(row_sem, peer(step, 0))
    halo_start(0)
    labels_along_y()

    spread_row, spread_col = iota((LANES, RANK), 0) % RANK, iota((LANES, RANK), 1)
    spread = one(spread_col == 4 * (spread_row % 8) + spread_row // 8, BF)

    def widen(c, carry):
        proj4[c] = dot(spread, proj_ref[c]).astype(BF)
        exp4[c] = jnp.concatenate([exp_ref[c]] * 4, axis=0)
        return carry

    with jax.named_scope("widen"):
        lax.fori_loop(0, cells, widen, 0, unroll=4)

    def project(layer, halves):
        lo, rows = halves[0] * half, len(halves) * half

        def body(c, carry):
            x = xe[layer, c // cells_y + 1, lax.rem(c, cells_y) + 1, lo : lo + rows, :]
            wide = dot_t(x, proj4[c])
            for n, h in enumerate(halves):
                top = wide[n * half : n * half + ROWS]
                low = wide[n * half + ROWS : (n + 1) * half]
                basis[h, c] = jnp.where(first_ch, top, low).astype(BF)
            return carry

        lax.fori_loop(0, cells, body, 0, unroll=8)

    with jax.named_scope("project"):
        project(0, (0, 1))

    to_scalars.wait()

    def send_one(r, step):
        o = lax.rem(me + step, count)
        pltpu.make_async_remote_copy(
            src_ref=out.at[r, o],
            dst_ref=inbox.at[r, me],
            send_sem=send_sem.at[r],
            recv_sem=recv_sem.at[r],
            device_id=(o // wide_y, lax.rem(o, wide_y)),
            device_id_type=MESH,
        ).start()

    def send_own(r):
        pltpu.make_async_copy(out.at[r, me], inbox.at[r, me], recv_sem.at[r]).start()

    group = 16

    def terms(rounds, halves):
        def body(n, carry):
            for d in range(group):
                o = lax.rem(me + n * group + d, count)
                s0, s1 = [lax.clamp(0, idx_s[k, 0, o], cells - 1) for k in range(2)]
                lhs = jnp.concatenate(
                    [jnp.where(first_slot, basis[h, s0], basis[h, s1]) for h in halves], axis=0
                )
                got = dot(lhs, wt[o]).astype(BF)
                for m, r in enumerate(rounds):
                    out[r, o] = got[m * ROWS : (m + 1) * ROWS]

            @pl.when(n == 0)
            def _():
                for r in rounds:
                    send_own(r)

            @pl.when(n > 0)
            def _():
                send_one(rounds[0], n * group)

            for d in range(1, group):
                send_one(rounds[0], n * group + d)
            return carry

        lax.fori_loop(0, count // group, body, 0)

    def send(r):
        def body(step, carry):
            send_one(r, step)
            return carry

        lax.fori_loop(1, count, body, 0)

    def receive(r):
        pltpu.make_async_copy(out.at[r], inbox.at[r], recv_sem.at[r]).wait()

    def near_field(layer):
        mix = mix_ref[layer]

        def body(c, carry):
            i, j = c // cells_y, lax.rem(c, cells_y)
            lhs = []
            for o in range(OFFSETS):
                active = mask_ref[i, j, o].astype(F32).astype(BF)
                lhs.append(xe[layer, i + o // 3, j + o % 3] * active)
            weights = tiles[pl.ds(c * OFFSETS, OFFSETS)].reshape(OFFSETS * LANES, LANES)
            near[c] = dot(jnp.concatenate(lhs, axis=1), weights) + dot(
                mix, xe[layer, i + 1, j + 1]
            )
            return carry

        lax.fori_loop(0, cells, body, 0, unroll=2)

    def gather(r):
        flat[: count * ROWS, :] = inbox[r].reshape(count * ROWS, LANES).astype(F32)
        chosen = sel[...]
        for row in range(ROWS):
            v = flat[pl.ds(row, count, stride=ROWS), :].astype(BF)
            got = dot(chosen, v)
            sums[pl.ds(row, cells, stride=ROWS), :] = got[:cells] + pltpu.roll(
                got[cells : 2 * cells], LANES - RANK, 1
            )

    def finish(layer, h):
        def body(c, carry):
            g = sums[pl.ds(c * ROWS, ROWS), :]
            lhs = jnp.concatenate(
                [jnp.where(first_slot & first_ch, g, 0.0), jnp.where(first_slot & ~first_ch, g, 0.0)],
                axis=0,
            ).astype(BF)
            hidden = near[c, h * half : (h + 1) * half, :] + dot(lhs, exp4[c])
            x = (gelu(hidden) * live[pl.ds(c, 1), :]).astype(BF)
            if layer + 1 < LAYERS:
                xe[layer + 1, c // cells_y + 1, lax.rem(c, cells_y) + 1, h * half : (h + 1) * half, :] = x
            else:
                res_ref[c, h * half : (h + 1) * half, :] = x
            return carry

        lax.fori_loop(0, cells, body, 0, unroll=4)

    scope = jax.named_scope
    with scope("barrier_all"):
        pl.semaphore_wait(row_sem, wide_x - 1)
    with scope("terms"):
        terms((0, 1), (0, 1))
    with scope("labels"):
        labels_along_x()
    with scope("send_terms"):
        send(1)
    with scope("wait_tiles"):
        for n in range(parts):
            tile_copy(n).wait()
    with scope("wait_halo"):
        halo_wait(0)
    with scope("near"):
        near_field(0)
    with scope("wait_labels"):
        some = pl.ds(0, count - wide_y)
        pltpu.make_async_copy(lab_turn.at[some], lab_in.at[some], lab_sem.at[3]).wait()
        sel[...] = jnp.transpose(lab_in[...])[: 2 * cells].astype(BF)
    for h in range(HALVES):
        with scope("wait_terms"):
            receive(h)
        with scope("gather"):
            gather(h)
        with scope("finish"):
            finish(0, h)
        with scope("halo"):
            halo_start(1 + h)
        with scope("project"):
            project(1, (h,))
        with scope("terms"):
            terms((2 + h,), (h,))
    with scope("wait_halo"):
        halo_wait(1)
        halo_wait(2)
    with scope("near"):
        near_field(1)
    for h in range(HALVES):
        with scope("wait_terms"):
            receive(2 + h)
        with scope("gather"):
            gather(2 + h)
        with scope("finish"):
            finish(1, h)

    rest = pl.ds(0, count - 1)
    for r in range(2 * LAYERS):
        pltpu.make_async_copy(out.at[r, rest], inbox.at[r, rest], send_sem.at[r]).wait()
    some = pl.ds(0, count - wide_x)
    pltpu.make_async_copy(lab_out.at[some], lab_mid.at[some], lab_sem.at[0]).wait()
    some = pl.ds(0, count - wide_y)
    pltpu.make_async_copy(lab_turn.at[some], lab_in.at[some], lab_sem.at[2]).wait()
    for part, (layer, rows) in enumerate(halo_parts):
        for n in range(len(links)):
            halo(layer, part, rows, n).wait_send()


def shards(
    features,
    cell_count,
    near_mask,
    near_tiles,
    projection_basis,
    expand_basis,
    far_source,
    far_owner,
    far_cell,
    distant_pair_matrix,
    mixing,
):
    cells_x, cells_y, chans, slots = features.shape
    rank = projection_basis.shape[2]
    cells = cells_x * cells_y
    pairs = far_source.shape[2]
    wide_x, wide_y = lax.axis_size("gx"), lax.axis_size("gy")
    count = wide_x * wide_y
    vmem = pl.BlockSpec(memory_space=pltpu.VMEM)
    hbm = pl.BlockSpec(memory_space=pltpu.HBM)
    rounds = 2 * LAYERS
    result = pl.pallas_call(
        functools.partial(kernel, wide_x, wide_y, cells_x, cells_y),
        out_shape=jax.ShapeDtypeStruct((cells, chans, slots), BF),
        in_specs=[hbm] * 11,
        out_specs=vmem,
        scratch_shapes=[
            pltpu.SMEM((cells_x, cells_y), jnp.int32),
            pltpu.SMEM((cells_x, cells_y, OFFSETS), jnp.int32),
            pltpu.VMEM((cells, chans, slots), BF),
            pltpu.VMEM((cells, rank, slots), BF),
            pltpu.VMEM((cells, rank, slots), BF),
            pltpu.VMEM((1, pairs), jnp.int32),
            pltpu.VMEM((1, pairs), jnp.int32),
            pltpu.VMEM((1, pairs), jnp.int32),
            pltpu.VMEM((pairs, rank * rank), BF),
            pltpu.VMEM((LAYERS, chans, chans), BF),
            pltpu.VMEM((cells, 4 * rank, slots), BF),
            pltpu.SemaphoreType.DMA((10,)),
            pltpu.VMEM((cells * OFFSETS, slots, slots), BF),
            pltpu.VMEM((count, LANES, LANES), BF),
            pltpu.VMEM((LAYERS, cells_x + 2, cells_y + 2, chans, slots), BF),
            pltpu.VMEM((HALVES, cells, ROWS, LANES), BF),
            pltpu.VMEM((rounds, count, ROWS, LANES), BF),
            pltpu.VMEM((rounds, count, ROWS, LANES), BF),
            pltpu.VMEM((count * ROWS + ROWS, LANES), F32),
            pltpu.VMEM((cells * ROWS + ROWS, LANES), F32),
            pltpu.VMEM((cells, 4 * rank, slots), BF),
            pltpu.VMEM((count, LANES), F32),
            pltpu.VMEM((count, LANES), F32),
            pltpu.VMEM((count, LANES), F32),
            pltpu.VMEM((count, LANES), F32),
            pltpu.VMEM((2 * cells, count), BF),
            pltpu.VMEM((2, 8, LANES), jnp.int32),
            pltpu.SMEM((2, 8, LANES), jnp.int32),
            pltpu.VMEM((cells, chans, slots), F32),
            pltpu.VMEM((cells, slots), F32),
            pltpu.SemaphoreType.DMA((4,)),
            pltpu.SemaphoreType.DMA,
            pltpu.SemaphoreType.DMA((rounds,)),
            pltpu.SemaphoreType.DMA((rounds,)),
            pltpu.SemaphoreType.DMA((3, 8)),
            pltpu.SemaphoreType.DMA((3, 8)),
            pltpu.SemaphoreType.DMA((4,)),
            pltpu.SemaphoreType.REGULAR,
        ],
        compiler_params=pltpu.CompilerParams(
            collective_id=0, has_side_effects=True, vmem_limit_bytes=56 << 20
        ),
    )(
        cell_count,
        near_mask,
        features.reshape(cells, chans, slots),
        near_tiles.reshape(cells * OFFSETS, slots, slots),
        projection_basis.reshape(cells, rank, slots),
        expand_basis.reshape(cells, rank, slots),
        far_source.reshape(1, pairs),
        far_owner.reshape(1, pairs),
        far_cell.reshape(1, pairs),
        distant_pair_matrix.reshape(pairs, rank * rank),
        mixing,
    )
    return result.reshape(cells_x, cells_y, chans, slots)


def solution(mesh):
    placed = (
        P("gx", "gy", None, None),
        P("gx", "gy"),
        P("gx", "gy", None),
        P("gx", "gy", None, None, None),
        P("gx", "gy", None, None),
        P("gx", "gy", None, None),
        P("gx", "gy", None),
        P("gx", "gy", None, None),
        P("gx", "gy", None),
        P("gx", "gy", None, None),
        P(),
    )
    return jax.shard_map(
        shards, mesh=mesh, in_specs=placed, out_specs=P("gx", "gy", None, None), check_vma=False
    )
```

```python
import functools

import jax
import jax.numpy as jnp
from jax import lax
from jax.experimental import pallas as pl
from jax.experimental.pallas import tpu as pltpu
from jax.sharding import PartitionSpec as P

LAYERS = 2
HALVES = 2
OFFSETS = 9
MESH = pl.DeviceIdType.MESH
BF = jnp.bfloat16
F32 = jnp.float32
ROWS = 16
LANES = 128
RANK = 32


def iota(shape, dim):
    return lax.broadcasted_iota(jnp.int32, shape, dim)


def one(condition, kind=F32):
    return jnp.where(condition, 1.0, 0.0).astype(kind)


def dot(a, b):
    return jnp.dot(a, b, preferred_element_type=F32)


def dot_t(a, b):
    return lax.dot_general(a, b, (((1,), (1,)), ((), ())), preferred_element_type=F32)


def gelu(v):
    return 0.5 * v * (1.0 + lax.erf(v * 0.7071067811865476))


def kernel(
    wide_x,
    wide_y,
    cells_x,
    cells_y,
    count_hbm,
    mask_hbm,
    feat_hbm,
    tiles_hbm,
    proj_hbm,
    exp_hbm,
    src_hbm,
    own_hbm,
    cell_hbm,
    pair_hbm,
    mix_hbm,
    res_hbm,
    res_ref,
    res_sem,
    count_ref,
    mask_ref,
    feat_ref,
    proj_ref,
    exp_ref,
    src_ref,
    own_ref,
    cell_ref,
    pair_ref,
    mix_ref,
    proj4,
    load_sem,
    tiles,
    wt,
    xe,
    basis,
    out,
    inbox,
    flat,
    sums,
    exp4,
    lab_out,
    lab_mid,
    lab_turn,
    lab_in,
    sel,
    idx,
    idx_s,
    near,
    live,
    tile_sem,
    idx_sem,
    send_sem,
    recv_sem,
    halo_send,
    halo_recv,
    lab_sem,
    row_sem,
):
    a, b = lax.axis_index("gx"), lax.axis_index("gy")
    count = wide_x * wide_y
    me = a * wide_y + b
    cells = cells_x * cells_y
    half = 2 * ROWS

    def peer(da, db):
        return lax.rem(a + da + wide_x, wide_x), lax.rem(b + db + wide_y, wide_y)

    def signal(sem, where):
        pl.semaphore_signal(sem, inc=1, device_id=where, device_id_type=MESH)

    loads = [
        pltpu.make_async_copy(hbm, ref, load_sem.at[n])
        for n, (hbm, ref) in enumerate(
            [
                (count_hbm, count_ref),
                (feat_hbm, feat_ref),
                (src_hbm, src_ref),
                (own_hbm, own_ref),
                (cell_hbm, cell_ref),
                (pair_hbm, pair_ref),
                (proj_hbm, proj_ref),
                (exp_hbm, exp_ref),
                (mask_hbm, mask_ref),
                (mix_hbm, mix_ref),
            ]
        )
    ]
    for load in loads:
        load.start()

    barrier = pltpu.get_barrier_semaphore()
    for step in range(1, wide_y):
        signal(barrier, peer(0, step))
    for step in range(1, wide_x):
        signal(barrier, peer(step, 0))

    parts = tile_sem.shape[0]
    size = cells * OFFSETS // parts

    def tile_copy(n):
        rows = pl.ds(n * size, size)
        return pltpu.make_async_copy(tiles_hbm.at[rows], tiles.at[rows], tile_sem.at[n])

    for n in range(parts):
        tile_copy(n).start()

    lane = iota((1, LANES), 1)
    slot_of = (lane // RANK) % 2
    first_slot = slot_of == 0
    first_ch = lane < 2 * RANK

    for load in loads[:2]:
        load.wait()

    def enter(c, carry):
        i, j = c // cells_y, lax.rem(c, cells_y)
        alive = one(lane < count_ref[i, j])
        live[pl.ds(c, 1), :] = alive
        xe[0, i + 1, j + 1] = (feat_ref[c].astype(F32) * alive).astype(BF)
        return carry

    with jax.named_scope("enter"):
        lax.fori_loop(0, cells, enter, 0, unroll=4)

    for load in loads[2:]:
        load.wait()
    owner = own_ref[0]
    named = one(iota((count, LANES), 0) == owner)
    before = dot(named.astype(BF), one(iota((LANES, LANES), 0) < iota((LANES, LANES), 1), BF))
    slot0 = jnp.where(before < 0.5, named, 0.0)
    slots = (slot0.astype(BF), (named - slot0).astype(BF))
    source = jnp.broadcast_to(src_ref[0], (8, LANES)).astype(F32).astype(BF)
    target = cell_ref[0]
    labels = jnp.zeros((count, LANES), F32)
    for k in range(2):
        idx[k] = dot_t(source, slots[k]).astype(jnp.int32)
        wanted = one(iota((LANES, LANES), 0) == target + k * cells, BF)
        labels = labels + dot_t(slots[k], wanted)
    by_row, by_col = iota((count, LANES), 0), iota((count, LANES), 1)
    by_column = one(by_col == by_row % wide_x * wide_y + by_row // wide_x, BF)
    lab_out[...] = dot(by_column, labels.astype(BF))
    to_scalars = pltpu.make_async_copy(idx, idx_s, idx_sem)
    to_scalars.start()

    for k in range(2):
        for j in range(RANK * RANK // LANES):
            flat[pl.ds(k * 8 + j, count, stride=ROWS), :] = dot(
                slots[k], pair_ref[:, j * LANES : (j + 1) * LANES]
            )
    fold_row, fold_col = iota((2 * LANES, LANES), 0), iota((2 * LANES, LANES), 1)
    fold = one(
        (fold_row % RANK == fold_col % RANK) & (fold_row // LANES == (fold_col // RANK) % 2), BF
    )
    quarter = [one(lane // RANK == q) for q in range(4)]
    quarter_bf = [q.astype(BF) for q in quarter]
    block = 8

    def place(n, carry):
        lhs = []
        for d in range(block):
            v = flat[pl.ds((n * block + d) * ROWS, ROWS), :]
            lhs.append(
                jnp.concatenate(
                    [
                        jnp.concatenate([v[k * 8 : k * 8 + 8] * q for q in quarter], axis=0)
                        for k in range(2)
                    ],
                    axis=1,
                )
            )
        got = dot(jnp.concatenate(lhs, axis=0).astype(BF), fold).astype(BF)
        for d in range(block):
            r = got[d * RANK : (d + 1) * RANK]
            for q in range(4):
                wt[n * block + d, q * RANK : (q + 1) * RANK, :] = r * quarter_bf[q]
        return carry

    with jax.named_scope("place"):
        lax.fori_loop(0, count // block, place, 0, unroll=4)

    links = [
        (1, 0, (cells_x, pl.ds(1, cells_y)), (0, pl.ds(1, cells_y))),
        (-1, 0, (1, pl.ds(1, cells_y)), (cells_x + 1, pl.ds(1, cells_y))),
        (0, 1, (pl.ds(1, cells_x), cells_y), (pl.ds(1, cells_x), 0)),
        (0, -1, (pl.ds(1, cells_x), 1), (pl.ds(1, cells_x), cells_y + 1)),
        (1, 1, (cells_x, cells_y), (0, 0)),
        (1, -1, (cells_x, 1), (0, cells_y + 1)),
        (-1, 1, (1, cells_y), (cells_x + 1, 0)),
        (-1, -1, (1, 1), (cells_x + 1, cells_y + 1)),
    ]

    def halo(layer, part, rows, n):
        da, db, (si, sj), (ti, tj) = links[n]
        return pltpu.make_async_remote_copy(
            src_ref=xe.at[layer, si, sj, rows],
            dst_ref=xe.at[layer, ti, tj, rows],
            send_sem=halo_send.at[part, n],
            recv_sem=halo_recv.at[part, n],
            device_id=peer(da, db),
            device_id_type=MESH,
        )

    everything = pl.ds(0, 2 * half)
    halo_parts = [(0, everything), (1, pl.ds(0, half)), (1, pl.ds(half, half))]

    def halo_start(part, some=range(8)):
        layer, rows = halo_parts[part]
        for n in some:
            halo(layer, part, rows, n).start()

    def halo_wait(part):
        layer, rows = halo_parts[part]
        for n in range(len(links)):
            halo(layer, part, rows, n).wait_recv()

    def labels_along_y():
        for step in range(1, wide_y):
            there = peer(0, step)
            pltpu.make_async_remote_copy(
                src_ref=lab_out.at[pl.ds(pl.multiple_of(there[1] * wide_x, wide_x), wide_x)],
                dst_ref=lab_mid.at[pl.ds(pl.multiple_of(b * wide_x, wide_x), wide_x)],
                send_sem=lab_sem.at[0],
                recv_sem=lab_sem.at[1],
                device_id=there,
                device_id_type=MESH,
            ).start()
        mine = pl.ds(pl.multiple_of(b * wide_x, wide_x), wide_x)
        lab_mid[mine, :] = lab_out[mine, :]

    def labels_along_x():
        some = pl.ds(0, count - wide_x)
        pltpu.make_async_copy(lab_out.at[some], lab_mid.at[some], lab_sem.at[1]).wait()
        lab_turn[...] = lax.dot_general(
            by_column,
            lab_mid[...].astype(BF),
            (((0,), (0,)), ((), ())),
            preferred_element_type=F32,
        )
        for step in range(1, wide_x):
            there = peer(step, 0)
            pltpu.make_async_remote_copy(
                src_ref=lab_turn.at[pl.ds(pl.multiple_of(there[0] * wide_y, wide_y), wide_y)],
                dst_ref=lab_in.at[pl.ds(pl.multiple_of(a * wide_y, wide_y), wide_y)],
                send_sem=lab_sem.at[2],
                recv_sem=lab_sem.at[3],
                device_id=there,
                device_id_type=MESH,
            ).start()
        mine = pl.ds(pl.multiple_of(a * wide_y, wide_y), wide_y)
        lab_in[mine, :] = lab_turn[mine, :]

    with jax.named_scope("barrier_near"):
        pl.semaphore_wait(barrier, wide_x + wide_y - 2)
    for step in range(1, wide_x):
        signal(row_sem, peer(step, 0))
    halo_start(0, range(4))
    labels_along_y()

    spread_row, spread_col = iota((LANES, RANK), 0) % RANK, iota((LANES, RANK), 1)
    spread = one(spread_col == 4 * (spread_row % 8) + spread_row // 8, BF)

    def widen(c, carry):
        proj4[c] = dot(spread, proj_ref[c]).astype(BF)
        exp4[c] = jnp.concatenate([exp_ref[c]] * 4, axis=0)
        return carry

    with jax.named_scope("widen"):
        lax.fori_loop(0, cells, widen, 0, unroll=4)

    def project(layer, halves):
        lo, rows = halves[0] * half, len(halves) * half

        def body(c, carry):
            x = xe[layer, c // cells_y + 1, lax.rem(c, cells_y) + 1, lo : lo + rows, :]
            wide = dot_t(x, proj4[c])
            for n, h in enumerate(halves):
                top = wide[n * half : n * half + ROWS]
                low = wide[n * half + ROWS : (n + 1) * half]
                basis[h, c] = jnp.where(first_ch, top, low).astype(BF)
            return carry

        lax.fori_loop(0, cells, body, 0, unroll=8)

    with jax.named_scope("project"):
        project(0, (0, 1))

    to_scalars.wait()

    def send_one(r, step):
        o = lax.rem(me + step, count)
        pltpu.make_async_remote_copy(
            src_ref=out.at[r, o],
            dst_ref=inbox.at[r, me],
            send_sem=send_sem.at[r],
            recv_sem=recv_sem.at[r],
            device_id=o,
            device_id_type=pl.DeviceIdType.LOGICAL,
        ).start()

    def send_own(r):
        pltpu.make_async_copy(out.at[r, me], inbox.at[r, me], recv_sem.at[r]).start()

    group = 8

    def terms(rounds, halves):
        def body(n, carry):
            for d in range(group):
                o = lax.rem(me + n * group + d, count)
                s0, s1 = [lax.clamp(0, idx_s[k, 0, o], cells - 1) for k in range(2)]
                lhs = jnp.concatenate(
                    [jnp.where(first_slot, basis[h, s0], basis[h, s1]) for h in halves], axis=0
                )
                got = dot(lhs, wt[o]).astype(BF)
                for m, r in enumerate(rounds):
                    out[r, o] = got[m * ROWS : (m + 1) * ROWS]

            @pl.when(n == 0)
            def _():
                for r in rounds:
                    send_own(r)

            @pl.when(n > 0)
            def _():
                send_one(rounds[0], n * group)

            for d in range(1, group):
                send_one(rounds[0], n * group + d)
            return carry

        lax.fori_loop(0, count // group, body, 0)

    def send(r):
        def body(n, carry):
            for d in range(group):
                send_one(r, n * group + d)
            return carry

        for d in range(1, group):
            send_one(r, d)
        lax.fori_loop(1, count // group, body, 0)

    def receive(r):
        pltpu.make_async_copy(out.at[r], inbox.at[r], recv_sem.at[r]).wait()

    def near_cells(layer, total, place_of):
        mix = mix_ref[layer]

        def body(n, carry):
            i, j = place_of(n)
            c = i * cells_y + j
            lhs = []
            for o in range(OFFSETS):
                active = mask_ref[i, j, o].astype(F32).astype(BF)
                lhs.append(xe[layer, i + o // 3, j + o % 3] * active)
            weights = tiles[pl.ds(c * OFFSETS, OFFSETS)].reshape(OFFSETS * LANES, LANES)
            near[c] = dot(jnp.concatenate(lhs, axis=1), weights) + dot(
                mix, xe[layer, i + 1, j + 1]
            )
            return carry

        lax.fori_loop(0, total, body, 0, unroll=4)

    def near_inner(layer):
        wide = cells_y - 2
        near_cells(
            layer, (cells_x - 2) * wide, lambda n: (1 + lax.div(n, wide), 1 + lax.rem(n, wide))
        )

    def near_edge(layer):
        near_cells(
            layer, 2 * cells_y, lambda n: (lax.div(n, cells_y) * (cells_x - 1), lax.rem(n, cells_y))
        )
        near_cells(
            layer, 2 * (cells_x - 2), lambda n: (1 + lax.div(n, 2), lax.rem(n, 2) * (cells_y - 1))
        )

    def gather(r):
        flat[: count * ROWS, :] = inbox[r].reshape(count * ROWS, LANES).astype(F32)
        chosen = sel[...]
        for row in range(ROWS):
            v = flat[pl.ds(row, count, stride=ROWS), :].astype(BF)
            got = dot(chosen, v)
            sums[pl.ds(row, cells, stride=ROWS), :] = got[:cells] + pltpu.roll(
                got[cells : 2 * cells], LANES - RANK, 1
            )

    def leave(h, n):
        where = (pl.ds(n * block, block), pl.ds(h * half, half))
        return pltpu.make_async_copy(res_ref.at[where], res_hbm.at[where], res_sem.at[h, n])

    def finish(layer, h):
        rows = slice(h * half, (h + 1) * half)

        def body(n, carry):
            for d in range(block):
                c = n * block + d
                g = sums[pl.ds(c * ROWS, ROWS), :]
                lhs = jnp.concatenate(
                    [
                        jnp.where(first_slot & first_ch, g, 0.0),
                        jnp.where(first_slot & ~first_ch, g, 0.0),
                    ],
                    axis=0,
                ).astype(BF)
                hidden = near[c, rows, :] + dot(lhs, exp4[c])
                x = (gelu(hidden) * live[pl.ds(c, 1), :]).astype(BF)
                if layer + 1 < LAYERS:
                    xe[layer + 1, c // cells_y + 1, lax.rem(c, cells_y) + 1, rows, :] = x
                else:
                    res_ref[c, rows, :] = x
            if layer + 1 == LAYERS:
                leave(h, n).start()
            return carry

        lax.fori_loop(0, cells // block, body, 0)

    scope = jax.named_scope
    with scope("barrier_all"):
        pl.semaphore_wait(row_sem, wide_x - 1)
        halo_start(0, range(4, 8))
    with scope("terms"):
        terms((0, 1), (0, 1))
    with scope("labels"):
        labels_along_x()
    with scope("send_terms"):
        send(1)
    with scope("wait_tiles"):
        for n in range(parts):
            tile_copy(n).wait()
    with scope("near"):
        near_inner(0)
    with scope("wait_halo"):
        halo_wait(0)
    with scope("near"):
        near_edge(0)
    with scope("wait_labels"):
        some = pl.ds(0, count - wide_y)
        pltpu.make_async_copy(lab_turn.at[some], lab_in.at[some], lab_sem.at[3]).wait()
        sel[...] = jnp.transpose(lab_in[...])[: 2 * cells].astype(BF)
    for h in range(HALVES):
        with scope("wait_terms"):
            receive(h)
        with scope("gather"):
            gather(h)
        with scope("finish"):
            finish(0, h)
        with scope("halo"):
            halo_start(1 + h)
        with scope("project"):
            project(1, (h,))
        with scope("terms"):
            terms((2 + h,), (h,))
    with scope("near"):
        near_inner(1)
    for h in range(HALVES):
        with scope("wait_terms"):
            receive(2 + h)
        with scope("gather"):
            gather(2 + h)
        if h == 0:
            with scope("wait_halo"):
                halo_wait(1)
                halo_wait(2)
            with scope("near"):
                near_edge(1)
        with scope("finish"):
            finish(1, h)

    for h in range(HALVES):
        for n in range(cells // block):
            leave(h, n).wait()
    rest = pl.ds(0, count - 1)
    for r in range(2 * LAYERS):
        pltpu.make_async_copy(out.at[r, rest], inbox.at[r, rest], send_sem.at[r]).wait()
    some = pl.ds(0, count - wide_x)
    pltpu.make_async_copy(lab_out.at[some], lab_mid.at[some], lab_sem.at[0]).wait()
    some = pl.ds(0, count - wide_y)
    pltpu.make_async_copy(lab_turn.at[some], lab_in.at[some], lab_sem.at[2]).wait()
    for part, (layer, rows) in enumerate(halo_parts):
        for n in range(len(links)):
            halo(layer, part, rows, n).wait_send()


def shards(
    features,
    cell_count,
    near_mask,
    near_tiles,
    projection_basis,
    expand_basis,
    far_source,
    far_owner,
    far_cell,
    distant_pair_matrix,
    mixing,
):
    cells_x, cells_y, chans, slots = features.shape
    rank = projection_basis.shape[2]
    cells = cells_x * cells_y
    pairs = far_source.shape[2]
    wide_x, wide_y = lax.axis_size("gx"), lax.axis_size("gy")
    count = wide_x * wide_y
    hbm = pl.BlockSpec(memory_space=pltpu.HBM)
    rounds = 2 * LAYERS
    result = pl.pallas_call(
        functools.partial(kernel, wide_x, wide_y, cells_x, cells_y),
        out_shape=jax.ShapeDtypeStruct((cells, chans, slots), BF),
        in_specs=[hbm] * 11,
        out_specs=hbm,
        scratch_shapes=[
            pltpu.VMEM((cells, chans, slots), BF),
            pltpu.SemaphoreType.DMA((HALVES, cells // 8)),
            pltpu.SMEM((cells_x, cells_y), jnp.int32),
            pltpu.SMEM((cells_x, cells_y, OFFSETS), jnp.int32),
            pltpu.VMEM((cells, chans, slots), BF),
            pltpu.VMEM((cells, rank, slots), BF),
            pltpu.VMEM((cells, rank, slots), BF),
            pltpu.VMEM((1, pairs), jnp.int32),
            pltpu.VMEM((1, pairs), jnp.int32),
            pltpu.VMEM((1, pairs), jnp.int32),
            pltpu.VMEM((pairs, rank * rank), BF),
            pltpu.VMEM((LAYERS, chans, chans), BF),
            pltpu.VMEM((cells, 4 * rank, slots), BF),
            pltpu.SemaphoreType.DMA((10,)),
            pltpu.VMEM((cells * OFFSETS, slots, slots), BF),
            pltpu.VMEM((count, LANES, LANES), BF),
            pltpu.VMEM((LAYERS, cells_x + 2, cells_y + 2, chans, slots), BF),
            pltpu.VMEM((HALVES, cells, ROWS, LANES), BF),
            pltpu.VMEM((rounds, count, ROWS, LANES), BF),
            pltpu.VMEM((rounds, count, ROWS, LANES), BF),
            pltpu.VMEM((count * ROWS + ROWS, LANES), F32),
            pltpu.VMEM((cells * ROWS + ROWS, LANES), F32),
            pltpu.VMEM((cells, 4 * rank, slots), BF),
            pltpu.VMEM((count, LANES), F32),
            pltpu.VMEM((count, LANES), F32),
            pltpu.VMEM((count, LANES), F32),
            pltpu.VMEM((count, LANES), F32),
            pltpu.VMEM((2 * cells, count), BF),
            pltpu.VMEM((2, 8, LANES), jnp.int32),
            pltpu.SMEM((2, 8, LANES), jnp.int32),
            pltpu.VMEM((cells, chans, slots), F32),
            pltpu.VMEM((cells, slots), F32),
            pltpu.SemaphoreType.DMA((4,)),
            pltpu.SemaphoreType.DMA,
            pltpu.SemaphoreType.DMA((rounds,)),
            pltpu.SemaphoreType.DMA((rounds,)),
            pltpu.SemaphoreType.DMA((3, 8)),
            pltpu.SemaphoreType.DMA((3, 8)),
            pltpu.SemaphoreType.DMA((4,)),
            pltpu.SemaphoreType.REGULAR,
        ],
        compiler_params=pltpu.CompilerParams(
            collective_id=0, has_side_effects=True, vmem_limit_bytes=56 << 20
        ),
    )(
        cell_count,
        near_mask,
        features.reshape(cells, chans, slots),
        near_tiles.reshape(cells * OFFSETS, slots, slots),
        projection_basis.reshape(cells, rank, slots),
        expand_basis.reshape(cells, rank, slots),
        far_source.reshape(1, pairs),
        far_owner.reshape(1, pairs),
        far_cell.reshape(1, pairs),
        distant_pair_matrix.reshape(pairs, rank * rank),
        mixing,
    )
    return result.reshape(cells_x, cells_y, chans, slots)


def solution(mesh):
    placed = (
        P("gx", "gy", None, None),
        P("gx", "gy"),
        P("gx", "gy", None),
        P("gx", "gy", None, None, None),
        P("gx", "gy", None, None),
        P("gx", "gy", None, None),
        P("gx", "gy", None),
        P("gx", "gy", None, None),
        P("gx", "gy", None),
        P("gx", "gy", None, None),
        P(),
    )
    return jax.shard_map(
        shards, mesh=mesh, in_specs=placed, out_specs=P("gx", "gy", None, None), check_vma=False
    )
```

```python
import functools

import jax
import jax.numpy as jnp
from jax import lax
from jax.experimental import pallas as pl
from jax.experimental.pallas import tpu as pltpu
from jax.sharding import PartitionSpec as P

LAYERS = 2
HALVES = 2
OFFSETS = 9
FLAT = pl.DeviceIdType.LOGICAL
BF = jnp.bfloat16
F32 = jnp.float32
ROWS = 16
LANES = 128
RANK = 32


def iota(shape, dim):
    return lax.broadcasted_iota(jnp.int32, shape, dim)


def one(condition, kind=F32):
    return jnp.where(condition, 1.0, 0.0).astype(kind)


def dot(a, b):
    return jnp.dot(a, b, preferred_element_type=F32)


def dot_t(a, b):
    return lax.dot_general(a, b, (((1,), (1,)), ((), ())), preferred_element_type=F32)


def gelu(v):
    return 0.5 * v * (1.0 + lax.erf(v * 0.7071067811865476))


def kernel(
    wide_x,
    wide_y,
    cells_x,
    cells_y,
    count_hbm,
    mask_hbm,
    feat_hbm,
    tiles_hbm,
    proj_hbm,
    exp_hbm,
    src_hbm,
    own_hbm,
    cell_hbm,
    pair_hbm,
    mix_hbm,
    res_hbm,
    res_ref,
    res_sem,
    count_ref,
    mask_ref,
    feat_ref,
    proj_ref,
    exp_ref,
    src_ref,
    own_ref,
    cell_ref,
    pair_ref,
    mix_ref,
    proj4,
    load_sem,
    tiles,
    wt,
    xe,
    basis,
    out,
    inbox,
    flat,
    sums,
    exp4,
    lab_out,
    lab_mid,
    lab_turn,
    lab_in,
    sel,
    idx,
    idx_s,
    near,
    live,
    tile_sem,
    idx_sem,
    send_sem,
    recv_sem,
    halo_send,
    halo_recv,
    lab_sem,
    row_sem,
):
    a, b = lax.axis_index("gx"), lax.axis_index("gy")
    count = wide_x * wide_y
    me = a * wide_y + b
    cells = cells_x * cells_y
    half = 2 * ROWS

    def peer(da, db):
        return lax.rem(a + da + wide_x, wide_x), lax.rem(b + db + wide_y, wide_y)

    def flat_id(where):
        return where[0] * wide_y + where[1]

    def signal(sem, where):
        pl.semaphore_signal(sem, inc=1, device_id=flat_id(where), device_id_type=FLAT)

    loads = [
        pltpu.make_async_copy(hbm, ref, load_sem.at[n])
        for n, (hbm, ref) in enumerate(
            [
                (count_hbm, count_ref),
                (feat_hbm, feat_ref),
                (src_hbm, src_ref),
                (own_hbm, own_ref),
                (cell_hbm, cell_ref),
                (pair_hbm, pair_ref),
                (proj_hbm, proj_ref),
                (exp_hbm, exp_ref),
                (mask_hbm, mask_ref),
                (mix_hbm, mix_ref),
            ]
        )
    ]
    for load in loads:
        load.start()

    barrier = pltpu.get_barrier_semaphore()
    for step in range(1, wide_y):
        signal(barrier, peer(0, step))
    for step in range(1, wide_x):
        signal(barrier, peer(step, 0))

    parts = tile_sem.shape[0]
    size = cells * OFFSETS // parts

    def tile_copy(n):
        rows = pl.ds(n * size, size)
        return pltpu.make_async_copy(tiles_hbm.at[rows], tiles.at[rows], tile_sem.at[n])

    for n in range(parts):
        tile_copy(n).start()

    lane = iota((1, LANES), 1)
    slot_of = (lane // RANK) % 2
    first_slot = slot_of == 0
    first_ch = lane < 2 * RANK

    for load in loads[:2]:
        load.wait()

    def enter(c, carry):
        i, j = c // cells_y, lax.rem(c, cells_y)
        alive = one(lane < count_ref[i, j])
        live[pl.ds(c, 1), :] = alive
        xe[0, i + 1, j + 1] = (feat_ref[c].astype(F32) * alive).astype(BF)
        return carry

    with jax.named_scope("enter"):
        lax.fori_loop(0, cells, enter, 0, unroll=4)

    for load in loads[2:]:
        load.wait()
    owner = own_ref[0]
    named = one(iota((count, LANES), 0) == owner)
    before = dot(named.astype(BF), one(iota((LANES, LANES), 0) < iota((LANES, LANES), 1), BF))
    slot0 = jnp.where(before < 0.5, named, 0.0)
    slots = (slot0.astype(BF), (named - slot0).astype(BF))
    source = jnp.broadcast_to(src_ref[0], (8, LANES)).astype(F32).astype(BF)
    target = cell_ref[0]
    labels = jnp.zeros((count, LANES), F32)
    for k in range(2):
        idx[k] = dot_t(source, slots[k]).astype(jnp.int32)
        wanted = one(iota((LANES, LANES), 0) == target + k * cells, BF)
        labels = labels + dot_t(slots[k], wanted)
    by_row, by_col = iota((count, LANES), 0), iota((count, LANES), 1)
    by_column = one(by_col == by_row % wide_x * wide_y + by_row // wide_x, BF)
    lab_out[...] = dot(by_column, labels.astype(BF))
    to_scalars = pltpu.make_async_copy(idx, idx_s, idx_sem)
    to_scalars.start()

    for k in range(2):
        for j in range(RANK * RANK // LANES):
            flat[pl.ds(k * 8 + j, count, stride=ROWS), :] = dot(
                slots[k], pair_ref[:, j * LANES : (j + 1) * LANES]
            )
    fold_row, fold_col = iota((2 * LANES, LANES), 0), iota((2 * LANES, LANES), 1)
    fold = one(
        (fold_row % RANK == fold_col % RANK) & (fold_row // LANES == (fold_col // RANK) % 2), BF
    )
    quarter = [one(lane // RANK == q) for q in range(4)]
    quarter_bf = [q.astype(BF) for q in quarter]
    block = 8

    def place(n, carry):
        lhs = []
        for d in range(block):
            v = flat[pl.ds((n * block + d) * ROWS, ROWS), :]
            lhs.append(
                jnp.concatenate(
                    [
                        jnp.concatenate([v[k * 8 : k * 8 + 8] * q for q in quarter], axis=0)
                        for k in range(2)
                    ],
                    axis=1,
                )
            )
        got = dot(jnp.concatenate(lhs, axis=0).astype(BF), fold).astype(BF)
        for d in range(block):
            r = got[d * RANK : (d + 1) * RANK]
            for q in range(4):
                wt[n * block + d, q * RANK : (q + 1) * RANK, :] = r * quarter_bf[q]
        return carry

    with jax.named_scope("place"):
        lax.fori_loop(0, count // block, place, 0, unroll=4)

    links = [
        (1, 0, (cells_x, pl.ds(1, cells_y)), (0, pl.ds(1, cells_y))),
        (-1, 0, (1, pl.ds(1, cells_y)), (cells_x + 1, pl.ds(1, cells_y))),
        (0, 1, (pl.ds(1, cells_x), cells_y), (pl.ds(1, cells_x), 0)),
        (0, -1, (pl.ds(1, cells_x), 1), (pl.ds(1, cells_x), cells_y + 1)),
        (1, 1, (cells_x, cells_y), (0, 0)),
        (1, -1, (cells_x, 1), (0, cells_y + 1)),
        (-1, 1, (1, cells_y), (cells_x + 1, 0)),
        (-1, -1, (1, 1), (cells_x + 1, cells_y + 1)),
    ]

    def halo(layer, part, rows, n):
        da, db, (si, sj), (ti, tj) = links[n]
        return pltpu.make_async_remote_copy(
            src_ref=xe.at[layer, si, sj, rows],
            dst_ref=xe.at[layer, ti, tj, rows],
            send_sem=halo_send.at[part, n],
            recv_sem=halo_recv.at[part, n],
            device_id=flat_id(peer(da, db)),
            device_id_type=FLAT,
        )

    everything = pl.ds(0, 2 * half)
    halo_parts = [(0, everything), (1, pl.ds(0, half)), (1, pl.ds(half, half))]

    def halo_start(part, some=range(8)):
        layer, rows = halo_parts[part]
        for n in some:
            halo(layer, part, rows, n).start()

    def halo_wait(part):
        layer, rows = halo_parts[part]
        for n in range(len(links)):
            halo(layer, part, rows, n).wait_recv()

    def labels_along_y():
        for step in range(1, wide_y):
            there = peer(0, step)
            pltpu.make_async_remote_copy(
                src_ref=lab_out.at[pl.ds(pl.multiple_of(there[1] * wide_x, wide_x), wide_x)],
                dst_ref=lab_mid.at[pl.ds(pl.multiple_of(b * wide_x, wide_x), wide_x)],
                send_sem=lab_sem.at[0],
                recv_sem=lab_sem.at[1],
                device_id=flat_id(there),
                device_id_type=FLAT,
            ).start()
        mine = pl.ds(pl.multiple_of(b * wide_x, wide_x), wide_x)
        lab_mid[mine, :] = lab_out[mine, :]

    def labels_along_x():
        some = pl.ds(0, count - wide_x)
        pltpu.make_async_copy(lab_out.at[some], lab_mid.at[some], lab_sem.at[1]).wait()
        lab_turn[...] = lax.dot_general(
            by_column,
            lab_mid[...].astype(BF),
            (((0,), (0,)), ((), ())),
            preferred_element_type=F32,
        )
        for step in range(1, wide_x):
            there = peer(step, 0)
            pltpu.make_async_remote_copy(
                src_ref=lab_turn.at[pl.ds(pl.multiple_of(there[0] * wide_y, wide_y), wide_y)],
                dst_ref=lab_in.at[pl.ds(pl.multiple_of(a * wide_y, wide_y), wide_y)],
                send_sem=lab_sem.at[2],
                recv_sem=lab_sem.at[3],
                device_id=flat_id(there),
                device_id_type=FLAT,
            ).start()
        mine = pl.ds(pl.multiple_of(a * wide_y, wide_y), wide_y)
        lab_in[mine, :] = lab_turn[mine, :]

    with jax.named_scope("barrier_near"):
        pl.semaphore_wait(barrier, wide_x + wide_y - 2)
    for step in range(1, wide_x):
        signal(row_sem, peer(step, 0))
    halo_start(0, range(4))
    labels_along_y()

    spread_row, spread_col = iota((LANES, RANK), 0) % RANK, iota((LANES, RANK), 1)
    spread = one(spread_col == 4 * (spread_row % 8) + spread_row // 8, BF)

    def widen(c, carry):
        proj4[c] = dot(spread, proj_ref[c]).astype(BF)
        exp4[c] = jnp.concatenate([exp_ref[c]] * 4, axis=0)
        return carry

    with jax.named_scope("widen"):
        lax.fori_loop(0, cells, widen, 0, unroll=4)

    def project(layer, halves):
        lo, rows = halves[0] * half, len(halves) * half

        def body(c, carry):
            x = xe[layer, c // cells_y + 1, lax.rem(c, cells_y) + 1, lo : lo + rows, :]
            wide = dot_t(x, proj4[c])
            for n, h in enumerate(halves):
                top = wide[n * half : n * half + ROWS]
                low = wide[n * half + ROWS : (n + 1) * half]
                basis[h, c] = jnp.where(first_ch, top, low).astype(BF)
            return carry

        lax.fori_loop(0, cells, body, 0, unroll=8)

    with jax.named_scope("project"):
        project(0, (0, 1))

    to_scalars.wait()

    def send_one(r, step):
        o = lax.rem(me + step, count)
        pltpu.make_async_remote_copy(
            src_ref=out.at[r, o],
            dst_ref=inbox.at[r, me],
            send_sem=send_sem.at[r],
            recv_sem=recv_sem.at[r],
            device_id=o,
            device_id_type=FLAT,
        ).start()

    def send_own(r):
        pltpu.make_async_copy(out.at[r, me], inbox.at[r, me], recv_sem.at[r]).start()

    group = 8

    def terms(rounds, halves):
        def body(n, carry):
            for d in range(group):
                o = lax.rem(me + n * group + d, count)
                s0, s1 = [lax.clamp(0, idx_s[k, 0, o], cells - 1) for k in range(2)]
                lhs = jnp.concatenate(
                    [jnp.where(first_slot, basis[h, s0], basis[h, s1]) for h in halves], axis=0
                )
                got = dot(lhs, wt[o]).astype(BF)
                for m, r in enumerate(rounds):
                    out[r, o] = got[m * ROWS : (m + 1) * ROWS]

            @pl.when(n == 0)
            def _():
                for r in rounds:
                    send_own(r)

            @pl.when(n > 0)
            def _():
                send_one(rounds[0], n * group)

            for d in range(1, group):
                send_one(rounds[0], n * group + d)
            return carry

        lax.fori_loop(0, count // group, body, 0, unroll=2)

    def send(r):
        def body(n, carry):
            for d in range(group):
                send_one(r, n * group + d)
            return carry

        for d in range(1, group):
            send_one(r, d)
        lax.fori_loop(1, count // group, body, 0)

    def receive(r):
        pltpu.make_async_copy(out.at[r], inbox.at[r], recv_sem.at[r]).wait()

    def near_cells(layer, total, place_of):
        mix = mix_ref[layer]

        def body(n, carry):
            i, j = place_of(n)
            c = i * cells_y + j
            lhs = []
            for o in range(OFFSETS):
                active = mask_ref[i, j, o].astype(F32).astype(BF)
                lhs.append(xe[layer, i + o // 3, j + o % 3] * active)
            weights = tiles[pl.ds(c * OFFSETS, OFFSETS)].reshape(OFFSETS * LANES, LANES)
            near[c] = dot(jnp.concatenate(lhs, axis=1), weights) + dot(
                mix, xe[layer, i + 1, j + 1]
            )
            return carry

        lax.fori_loop(0, total, body, 0, unroll=4)

    def near_inner(layer):
        wide = cells_y - 2
        near_cells(
            layer, (cells_x - 2) * wide, lambda n: (1 + lax.div(n, wide), 1 + lax.rem(n, wide))
        )

    def near_edge(layer):
        near_cells(
            layer, 2 * cells_y, lambda n: (lax.div(n, cells_y) * (cells_x - 1), lax.rem(n, cells_y))
        )
        near_cells(
            layer, 2 * (cells_x - 2), lambda n: (1 + lax.div(n, 2), lax.rem(n, 2) * (cells_y - 1))
        )

    def gather(r):
        flat[: count * ROWS, :] = inbox[r].reshape(count * ROWS, LANES).astype(F32)
        chosen = sel[...]
        for row in range(ROWS):
            v = flat[pl.ds(row, count, stride=ROWS), :].astype(BF)
            got = dot(chosen, v)
            sums[pl.ds(row, cells, stride=ROWS), :] = got[:cells] + pltpu.roll(
                got[cells : 2 * cells], LANES - RANK, 1
            )

    def leave(h, n):
        where = (pl.ds(n * block, block), pl.ds(h * half, half))
        return pltpu.make_async_copy(res_ref.at[where], res_hbm.at[where], res_sem.at[h, n])

    def finish(layer, h):
        rows = slice(h * half, (h + 1) * half)

        def body(n, carry):
            for d in range(block):
                c = n * block + d
                g = sums[pl.ds(c * ROWS, ROWS), :]
                lhs = jnp.concatenate(
                    [
                        jnp.where(first_slot & first_ch, g, 0.0),
                        jnp.where(first_slot & ~first_ch, g, 0.0),
                    ],
                    axis=0,
                ).astype(BF)
                hidden = near[c, rows, :] + dot(lhs, exp4[c])
                x = (gelu(hidden) * live[pl.ds(c, 1), :]).astype(BF)
                if layer + 1 < LAYERS:
                    xe[layer + 1, c // cells_y + 1, lax.rem(c, cells_y) + 1, rows, :] = x
                else:
                    res_ref[c, rows, :] = x
            if layer + 1 == LAYERS:
                leave(h, n).start()
            return carry

        lax.fori_loop(0, cells // block, body, 0, unroll=2)

    scope = jax.named_scope
    with scope("barrier_all"):
        pl.semaphore_wait(row_sem, wide_x - 1)
        halo_start(0, range(4, 8))
    with scope("terms"):
        terms((0, 1), (0, 1))
    with scope("labels"):
        labels_along_x()
    with scope("send_terms"):
        send(1)
    with scope("wait_tiles"):
        for n in range(parts):
            tile_copy(n).wait()
    with scope("near"):
        near_inner(0)
    with scope("wait_halo"):
        halo_wait(0)
    with scope("near"):
        near_edge(0)
    with scope("wait_labels"):
        some = pl.ds(0, count - wide_y)
        pltpu.make_async_copy(lab_turn.at[some], lab_in.at[some], lab_sem.at[3]).wait()
        sel[...] = jnp.transpose(lab_in[...])[: 2 * cells].astype(BF)
    for h in range(HALVES):
        with scope("wait_terms"):
            receive(h)
        with scope("gather"):
            gather(h)
        with scope("finish"):
            finish(0, h)
        with scope("halo"):
            halo_start(1 + h)
        with scope("project"):
            project(1, (h,))
        with scope("terms"):
            terms((2 + h,), (h,))
    with scope("near"):
        near_inner(1)
    for h in range(HALVES):
        with scope("wait_terms"):
            receive(2 + h)
        with scope("gather"):
            gather(2 + h)
        if h == 0:
            with scope("wait_halo"):
                halo_wait(1)
                halo_wait(2)
            with scope("near"):
                near_edge(1)
        with scope("finish"):
            finish(1, h)

    for h in range(HALVES):
        for n in range(cells // block):
            leave(h, n).wait()
    rest = pl.ds(0, count - 1)
    for r in range(2 * LAYERS):
        pltpu.make_async_copy(out.at[r, rest], inbox.at[r, rest], send_sem.at[r]).wait()
    some = pl.ds(0, count - wide_x)
    pltpu.make_async_copy(lab_out.at[some], lab_mid.at[some], lab_sem.at[0]).wait()
    some = pl.ds(0, count - wide_y)
    pltpu.make_async_copy(lab_turn.at[some], lab_in.at[some], lab_sem.at[2]).wait()
    for part, (layer, rows) in enumerate(halo_parts):
        for n in range(len(links)):
            halo(layer, part, rows, n).wait_send()


def shards(
    features,
    cell_count,
    near_mask,
    near_tiles,
    projection_basis,
    expand_basis,
    far_source,
    far_owner,
    far_cell,
    distant_pair_matrix,
    mixing,
):
    cells_x, cells_y, chans, slots = features.shape
    rank = projection_basis.shape[2]
    cells = cells_x * cells_y
    pairs = far_source.shape[2]
    wide_x, wide_y = lax.axis_size("gx"), lax.axis_size("gy")
    count = wide_x * wide_y
    hbm = pl.BlockSpec(memory_space=pltpu.HBM)
    rounds = 2 * LAYERS
    result = pl.pallas_call(
        functools.partial(kernel, wide_x, wide_y, cells_x, cells_y),
        out_shape=jax.ShapeDtypeStruct((cells, chans, slots), BF),
        in_specs=[hbm] * 11,
        out_specs=hbm,
        scratch_shapes=[
            pltpu.VMEM((cells, chans, slots), BF),
            pltpu.SemaphoreType.DMA((HALVES, cells // 8)),
            pltpu.SMEM((cells_x, cells_y), jnp.int32),
            pltpu.SMEM((cells_x, cells_y, OFFSETS), jnp.int32),
            pltpu.VMEM((cells, chans, slots), BF),
            pltpu.VMEM((cells, rank, slots), BF),
            pltpu.VMEM((cells, rank, slots), BF),
            pltpu.VMEM((1, pairs), jnp.int32),
            pltpu.VMEM((1, pairs), jnp.int32),
            pltpu.VMEM((1, pairs), jnp.int32),
            pltpu.VMEM((pairs, rank * rank), BF),
            pltpu.VMEM((LAYERS, chans, chans), BF),
            pltpu.VMEM((cells, 4 * rank, slots), BF),
            pltpu.SemaphoreType.DMA((10,)),
            pltpu.VMEM((cells * OFFSETS, slots, slots), BF),
            pltpu.VMEM((count, LANES, LANES), BF),
            pltpu.VMEM((LAYERS, cells_x + 2, cells_y + 2, chans, slots), BF),
            pltpu.VMEM((HALVES, cells, ROWS, LANES), BF),
            pltpu.VMEM((rounds, count, ROWS, LANES), BF),
            pltpu.VMEM((rounds, count, ROWS, LANES), BF),
            pltpu.VMEM((count * ROWS + ROWS, LANES), F32),
            pltpu.VMEM((cells * ROWS + ROWS, LANES), F32),
            pltpu.VMEM((cells, 4 * rank, slots), BF),
            pltpu.VMEM((count, LANES), F32),
            pltpu.VMEM((count, LANES), F32),
            pltpu.VMEM((count, LANES), F32),
            pltpu.VMEM((count, LANES), F32),
            pltpu.VMEM((2 * cells, count), BF),
            pltpu.VMEM((2, 8, LANES), jnp.int32),
            pltpu.SMEM((2, 8, LANES), jnp.int32),
            pltpu.VMEM((cells, chans, slots), F32),
            pltpu.VMEM((cells, slots), F32),
            pltpu.SemaphoreType.DMA((4,)),
            pltpu.SemaphoreType.DMA,
            pltpu.SemaphoreType.DMA((rounds,)),
            pltpu.SemaphoreType.DMA((rounds,)),
            pltpu.SemaphoreType.DMA((3, 8)),
            pltpu.SemaphoreType.DMA((3, 8)),
            pltpu.SemaphoreType.DMA((4,)),
            pltpu.SemaphoreType.REGULAR,
        ],
        compiler_params=pltpu.CompilerParams(
            collective_id=0, has_side_effects=True, vmem_limit_bytes=56 << 20
        ),
    )(
        cell_count,
        near_mask,
        features.reshape(cells, chans, slots),
        near_tiles.reshape(cells * OFFSETS, slots, slots),
        projection_basis.reshape(cells, rank, slots),
        expand_basis.reshape(cells, rank, slots),
        far_source.reshape(1, pairs),
        far_owner.reshape(1, pairs),
        far_cell.reshape(1, pairs),
        distant_pair_matrix.reshape(pairs, rank * rank),
        mixing,
    )
    return result.reshape(cells_x, cells_y, chans, slots)


def solution(mesh):
    placed = (
        P("gx", "gy", None, None),
        P("gx", "gy"),
        P("gx", "gy", None),
        P("gx", "gy", None, None, None),
        P("gx", "gy", None, None),
        P("gx", "gy", None, None),
        P("gx", "gy", None),
        P("gx", "gy", None, None),
        P("gx", "gy", None),
        P("gx", "gy", None, None),
        P(),
    )
    return jax.shard_map(
        shards, mesh=mesh, in_specs=placed, out_specs=P("gx", "gy", None, None), check_vma=False
    )
```

```python
import functools

import jax
import jax.numpy as jnp
from jax import lax
from jax.experimental import pallas as pl
from jax.experimental.pallas import tpu as pltpu
from jax.sharding import PartitionSpec as P

LAYERS = 2
HALVES = 2
OFFSETS = 9
FLAT = pl.DeviceIdType.LOGICAL
BF = jnp.bfloat16
F32 = jnp.float32
ROWS = 16
LANES = 128
RANK = 32


def iota(shape, dim):
    return lax.broadcasted_iota(jnp.int32, shape, dim)


def one(condition, kind=F32):
    return jnp.where(condition, 1.0, 0.0).astype(kind)


def dot(a, b):
    return jnp.dot(a, b, preferred_element_type=F32)


def dot_t(a, b):
    return lax.dot_general(a, b, (((1,), (1,)), ((), ())), preferred_element_type=F32)


def gelu(v):
    return 0.5 * v * (1.0 + lax.erf(v * 0.7071067811865476))


def kernel(
    wide_x,
    wide_y,
    cells_x,
    cells_y,
    count_hbm,
    mask_hbm,
    feat_hbm,
    tiles_hbm,
    proj_hbm,
    exp_hbm,
    src_hbm,
    own_hbm,
    cell_hbm,
    pair_hbm,
    mix_hbm,
    res_hbm,
    res_ref,
    res_sem,
    count_ref,
    mask_ref,
    feat_ref,
    proj_ref,
    exp_ref,
    src_ref,
    own_ref,
    cell_ref,
    pair_ref,
    mix_ref,
    proj4,
    load_sem,
    tiles,
    wt,
    xe,
    basis,
    out,
    inbox,
    flat,
    sums,
    exp4,
    lab_out,
    lab_mid,
    lab_turn,
    lab_in,
    sel,
    idx,
    idx_s,
    near,
    live,
    tile_sem,
    idx_sem,
    send_sem,
    recv_sem,
    halo_send,
    halo_recv,
    lab_sem,
    row_sem,
):
    a, b = lax.axis_index("gx"), lax.axis_index("gy")
    count = wide_x * wide_y
    me = a * wide_y + b
    cells = cells_x * cells_y
    half = 2 * ROWS

    def peer(da, db):
        return lax.rem(a + da + wide_x, wide_x), lax.rem(b + db + wide_y, wide_y)

    def flat_id(where):
        return where[0] * wide_y + where[1]

    def signal(sem, where):
        pl.semaphore_signal(sem, inc=1, device_id=flat_id(where), device_id_type=FLAT)

    loads = [
        pltpu.make_async_copy(hbm, ref, load_sem.at[n])
        for n, (hbm, ref) in enumerate(
            [
                (count_hbm, count_ref),
                (feat_hbm, feat_ref),
                (src_hbm, src_ref),
                (own_hbm, own_ref),
                (cell_hbm, cell_ref),
                (pair_hbm, pair_ref),
                (proj_hbm, proj_ref),
                (exp_hbm, exp_ref),
                (mask_hbm, mask_ref),
                (mix_hbm, mix_ref),
            ]
        )
    ]
    for load in loads:
        load.start()

    barrier = pltpu.get_barrier_semaphore()
    for step in range(1, wide_y):
        signal(barrier, peer(0, step))
    for step in range(1, wide_x):
        signal(barrier, peer(step, 0))

    parts = tile_sem.shape[0]
    size = cells * OFFSETS // parts

    def tile_copy(n):
        rows = pl.ds(n * size, size)
        return pltpu.make_async_copy(tiles_hbm.at[rows], tiles.at[rows], tile_sem.at[n])

    for n in range(parts):
        tile_copy(n).start()

    lane = iota((1, LANES), 1)
    slot_of = (lane // RANK) % 2
    first_slot = slot_of == 0
    first_ch = lane < 2 * RANK

    for load in loads[:2]:
        load.wait()

    def enter(c, carry):
        i, j = c // cells_y, lax.rem(c, cells_y)
        alive = one(lane < count_ref[i, j])
        live[pl.ds(c, 1), :] = alive
        xe[0, i + 1, j + 1] = (feat_ref[c].astype(F32) * alive).astype(BF)
        return carry

    with jax.named_scope("enter"):
        lax.fori_loop(0, cells, enter, 0, unroll=4)

    for load in loads[2:]:
        load.wait()
    owner = own_ref[0]
    named = one(iota((count, LANES), 0) == owner)
    before = dot(named.astype(BF), one(iota((LANES, LANES), 0) < iota((LANES, LANES), 1), BF))
    slot0 = jnp.where(before < 0.5, named, 0.0)
    slots = (slot0.astype(BF), (named - slot0).astype(BF))
    source = jnp.broadcast_to(src_ref[0], (8, LANES)).astype(F32).astype(BF)
    target = cell_ref[0]
    labels = jnp.zeros((count, LANES), F32)
    for k in range(2):
        idx[k] = dot_t(source, slots[k]).astype(jnp.int32)
        wanted = one(iota((LANES, LANES), 0) == target + k * cells, BF)
        labels = labels + dot_t(slots[k], wanted)
    by_row, by_col = iota((count, LANES), 0), iota((count, LANES), 1)
    by_column = one(by_col == by_row % wide_x * wide_y + by_row // wide_x, BF)
    lab_out[...] = dot(by_column, labels.astype(BF))
    to_scalars = pltpu.make_async_copy(idx, idx_s, idx_sem)
    to_scalars.start()

    for k in range(2):
        for j in range(RANK * RANK // LANES):
            flat[pl.ds(k * 8 + j, count, stride=ROWS), :] = dot(
                slots[k], pair_ref[:, j * LANES : (j + 1) * LANES]
            )
    fold_row, fold_col = iota((2 * LANES, LANES), 0), iota((2 * LANES, LANES), 1)
    fold = one(
        (fold_row % RANK == fold_col % RANK) & (fold_row // LANES == (fold_col // RANK) % 2), BF
    )
    quarter = [one(lane // RANK == q) for q in range(4)]
    quarter_bf = [q.astype(BF) for q in quarter]
    block = 8

    def place(n, carry):
        lhs = []
        for d in range(block):
            v = flat[pl.ds((n * block + d) * ROWS, ROWS), :]
            lhs.append(
                jnp.concatenate(
                    [
                        jnp.concatenate([v[k * 8 : k * 8 + 8] * q for q in quarter], axis=0)
                        for k in range(2)
                    ],
                    axis=1,
                )
            )
        got = dot(jnp.concatenate(lhs, axis=0).astype(BF), fold).astype(BF)
        for d in range(block):
            r = got[d * RANK : (d + 1) * RANK]
            for q in range(4):
                wt[n * block + d, q * RANK : (q + 1) * RANK, :] = r * quarter_bf[q]
        return carry

    with jax.named_scope("place"):
        lax.fori_loop(0, count // block, place, 0, unroll=4)

    links = [
        (1, 0, (cells_x, pl.ds(1, cells_y)), (0, pl.ds(1, cells_y))),
        (-1, 0, (1, pl.ds(1, cells_y)), (cells_x + 1, pl.ds(1, cells_y))),
        (0, 1, (pl.ds(1, cells_x), cells_y), (pl.ds(1, cells_x), 0)),
        (0, -1, (pl.ds(1, cells_x), 1), (pl.ds(1, cells_x), cells_y + 1)),
        (1, 1, (cells_x, cells_y), (0, 0)),
        (1, -1, (cells_x, 1), (0, cells_y + 1)),
        (-1, 1, (1, cells_y), (cells_x + 1, 0)),
        (-1, -1, (1, 1), (cells_x + 1, cells_y + 1)),
    ]

    def halo(layer, part, rows, n):
        da, db, (si, sj), (ti, tj) = links[n]
        return pltpu.make_async_remote_copy(
            src_ref=xe.at[layer, si, sj, rows],
            dst_ref=xe.at[layer, ti, tj, rows],
            send_sem=halo_send.at[part, n],
            recv_sem=halo_recv.at[part, n],
            device_id=flat_id(peer(da, db)),
            device_id_type=FLAT,
        )

    everything = pl.ds(0, 2 * half)
    halo_parts = [(0, everything), (1, pl.ds(0, half)), (1, pl.ds(half, half))]

    def halo_start(part, some=range(8)):
        layer, rows = halo_parts[part]
        for n in some:
            halo(layer, part, rows, n).start()

    def halo_wait(part):
        layer, rows = halo_parts[part]
        for n in range(len(links)):
            halo(layer, part, rows, n).wait_recv()

    def labels_along_y():
        for step in range(1, wide_y):
            there = peer(0, step)
            pltpu.make_async_remote_copy(
                src_ref=lab_out.at[pl.ds(pl.multiple_of(there[1] * wide_x, wide_x), wide_x)],
                dst_ref=lab_mid.at[pl.ds(pl.multiple_of(b * wide_x, wide_x), wide_x)],
                send_sem=lab_sem.at[0],
                recv_sem=lab_sem.at[1],
                device_id=flat_id(there),
                device_id_type=FLAT,
            ).start()
        mine = pl.ds(pl.multiple_of(b * wide_x, wide_x), wide_x)
        lab_mid[mine, :] = lab_out[mine, :]

    def labels_along_x():
        some = pl.ds(0, count - wide_x)
        pltpu.make_async_copy(lab_out.at[some], lab_mid.at[some], lab_sem.at[1]).wait()
        lab_turn[...] = lax.dot_general(
            by_column,
            lab_mid[...].astype(BF),
            (((0,), (0,)), ((), ())),
            preferred_element_type=F32,
        )
        for step in range(1, wide_x):
            there = peer(step, 0)
            pltpu.make_async_remote_copy(
                src_ref=lab_turn.at[pl.ds(pl.multiple_of(there[0] * wide_y, wide_y), wide_y)],
                dst_ref=lab_in.at[pl.ds(pl.multiple_of(a * wide_y, wide_y), wide_y)],
                send_sem=lab_sem.at[2],
                recv_sem=lab_sem.at[3],
                device_id=flat_id(there),
                device_id_type=FLAT,
            ).start()
        mine = pl.ds(pl.multiple_of(a * wide_y, wide_y), wide_y)
        lab_in[mine, :] = lab_turn[mine, :]

    with jax.named_scope("barrier_near"):
        pl.semaphore_wait(barrier, wide_x + wide_y - 2)
    for step in range(1, wide_x):
        signal(row_sem, peer(step, 0))
    halo_start(0, range(4))
    labels_along_y()

    spread_row, spread_col = iota((LANES, RANK), 0) % RANK, iota((LANES, RANK), 1)
    spread = one(spread_col == 4 * (spread_row % 8) + spread_row // 8, BF)

    def widen(c, carry):
        proj4[c] = dot(spread, proj_ref[c]).astype(BF)
        exp4[c] = jnp.concatenate([exp_ref[c]] * 4, axis=0)
        return carry

    with jax.named_scope("widen"):
        lax.fori_loop(0, cells, widen, 0, unroll=4)

    def project(layer, halves):
        lo, rows = halves[0] * half, len(halves) * half

        def body(c, carry):
            x = xe[layer, c // cells_y + 1, lax.rem(c, cells_y) + 1, lo : lo + rows, :]
            wide = dot_t(x, proj4[c])
            for n, h in enumerate(halves):
                top = wide[n * half : n * half + ROWS]
                low = wide[n * half + ROWS : (n + 1) * half]
                basis[h, c] = jnp.where(first_ch, top, low).astype(BF)
            return carry

        lax.fori_loop(0, cells, body, 0, unroll=16)

    with jax.named_scope("project"):
        project(0, (0, 1))

    to_scalars.wait()

    def send_one(r, step):
        o = lax.rem(me + step, count)
        pltpu.make_async_remote_copy(
            src_ref=out.at[r, o],
            dst_ref=inbox.at[r, me],
            send_sem=send_sem.at[r],
            recv_sem=recv_sem.at[r],
            device_id=o,
            device_id_type=FLAT,
        ).start()

    def send_own(r):
        pltpu.make_async_copy(out.at[r, me], inbox.at[r, me], recv_sem.at[r]).start()

    group = 8

    def terms(rounds, halves):
        def body(n, carry):
            for d in range(group):
                o = lax.rem(me + n * group + d, count)
                s0, s1 = [lax.clamp(0, idx_s[k, 0, o], cells - 1) for k in range(2)]
                lhs = jnp.concatenate(
                    [jnp.where(first_slot, basis[h, s0], basis[h, s1]) for h in halves], axis=0
                )
                got = dot(lhs, wt[o]).astype(BF)
                for m, r in enumerate(rounds):
                    out[r, o] = got[m * ROWS : (m + 1) * ROWS]

            @pl.when(n == 0)
            def _():
                for r in rounds:
                    send_own(r)

            @pl.when(n > 0)
            def _():
                send_one(rounds[0], n * group)

            for d in range(1, group):
                send_one(rounds[0], n * group + d)
            return carry

        lax.fori_loop(0, count // group, body, 0, unroll=2)

    def send(r):
        def body(n, carry):
            for d in range(group):
                send_one(r, n * group + d)
            return carry

        for d in range(1, group):
            send_one(r, d)
        lax.fori_loop(1, count // group, body, 0)

    def receive(r):
        pltpu.make_async_copy(out.at[r], inbox.at[r], recv_sem.at[r]).wait()

    def near_cells(layer, total, place_of):
        mix = mix_ref[layer]

        def body(n, carry):
            i, j = place_of(n)
            c = i * cells_y + j
            lhs = []
            for o in range(OFFSETS):
                active = mask_ref[i, j, o].astype(F32).astype(BF)
                lhs.append(xe[layer, i + o // 3, j + o % 3] * active)
            weights = tiles[pl.ds(c * OFFSETS, OFFSETS)].reshape(OFFSETS * LANES, LANES)
            near[c] = dot(jnp.concatenate(lhs, axis=1), weights) + dot(
                mix, xe[layer, i + 1, j + 1]
            )
            return carry

        lax.fori_loop(0, total, body, 0, unroll=4)

    def near_inner(layer):
        wide = cells_y - 2
        near_cells(
            layer, (cells_x - 2) * wide, lambda n: (1 + lax.div(n, wide), 1 + lax.rem(n, wide))
        )

    def near_edge(layer):
        near_cells(
            layer, 2 * cells_y, lambda n: (lax.div(n, cells_y) * (cells_x - 1), lax.rem(n, cells_y))
        )
        near_cells(
            layer, 2 * (cells_x - 2), lambda n: (1 + lax.div(n, 2), lax.rem(n, 2) * (cells_y - 1))
        )

    def gather(r):
        flat[: count * ROWS, :] = inbox[r].reshape(count * ROWS, LANES).astype(F32)
        chosen = sel[...]
        for row in range(ROWS):
            v = flat[pl.ds(row, count, stride=ROWS), :].astype(BF)
            got = dot(chosen, v)
            sums[pl.ds(row, cells, stride=ROWS), :] = got[:cells] + pltpu.roll(
                got[cells : 2 * cells], LANES - RANK, 1
            )

    def leave(h, n):
        where = (pl.ds(n * block, block), pl.ds(h * half, half))
        return pltpu.make_async_copy(res_ref.at[where], res_hbm.at[where], res_sem.at[h, n])

    def finish(layer, h):
        rows = slice(h * half, (h + 1) * half)

        def body(n, carry):
            for d in range(block):
                c = n * block + d
                g = sums[pl.ds(c * ROWS, ROWS), :]
                lhs = jnp.concatenate(
                    [
                        jnp.where(first_slot & first_ch, g, 0.0),
                        jnp.where(first_slot & ~first_ch, g, 0.0),
                    ],
                    axis=0,
                ).astype(BF)
                hidden = near[c, rows, :] + dot(lhs, exp4[c])
                x = (gelu(hidden) * live[pl.ds(c, 1), :]).astype(BF)
                if layer + 1 < LAYERS:
                    xe[layer + 1, c // cells_y + 1, lax.rem(c, cells_y) + 1, rows, :] = x
                else:
                    res_ref[c, rows, :] = x
            if layer + 1 == LAYERS:
                leave(h, n).start()
            return carry

        lax.fori_loop(0, cells // block, body, 0, unroll=4)

    scope = jax.named_scope
    with scope("barrier_all"):
        pl.semaphore_wait(row_sem, wide_x - 1)
        halo_start(0, range(4, 8))
    with scope("terms"):
        terms((0, 1), (0, 1))
    with scope("labels"):
        labels_along_x()
    with scope("send_terms"):
        send(1)
    with scope("wait_tiles"):
        for n in range(parts):
            tile_copy(n).wait()
    with scope("near"):
        near_inner(0)
    with scope("wait_halo"):
        halo_wait(0)
    with scope("near"):
        near_edge(0)
    with scope("wait_labels"):
        some = pl.ds(0, count - wide_y)
        pltpu.make_async_copy(lab_turn.at[some], lab_in.at[some], lab_sem.at[3]).wait()
        sel[...] = jnp.transpose(lab_in[...])[: 2 * cells].astype(BF)
    for h in range(HALVES):
        with scope("wait_terms"):
            receive(h)
        with scope("gather"):
            gather(h)
        with scope("finish"):
            finish(0, h)
        with scope("halo"):
            halo_start(1 + h)
        with scope("project"):
            project(1, (h,))
        with scope("terms"):
            terms((2 + h,), (h,))
    with scope("near"):
        near_inner(1)
    for h in range(HALVES):
        with scope("wait_terms"):
            receive(2 + h)
        with scope("gather"):
            gather(2 + h)
        if h == 0:
            with scope("wait_halo"):
                halo_wait(1)
                halo_wait(2)
            with scope("near"):
                near_edge(1)
        with scope("finish"):
            finish(1, h)

    for h in range(HALVES):
        for n in range(cells // block):
            leave(h, n).wait()
    rest = pl.ds(0, count - 1)
    for r in range(2 * LAYERS):
        pltpu.make_async_copy(out.at[r, rest], inbox.at[r, rest], send_sem.at[r]).wait()
    some = pl.ds(0, count - wide_x)
    pltpu.make_async_copy(lab_out.at[some], lab_mid.at[some], lab_sem.at[0]).wait()
    some = pl.ds(0, count - wide_y)
    pltpu.make_async_copy(lab_turn.at[some], lab_in.at[some], lab_sem.at[2]).wait()
    for part, (layer, rows) in enumerate(halo_parts):
        for n in range(len(links)):
            halo(layer, part, rows, n).wait_send()


def shards(
    features,
    cell_count,
    near_mask,
    near_tiles,
    projection_basis,
    expand_basis,
    far_source,
    far_owner,
    far_cell,
    distant_pair_matrix,
    mixing,
):
    cells_x, cells_y, chans, slots = features.shape
    rank = projection_basis.shape[2]
    cells = cells_x * cells_y
    pairs = far_source.shape[2]
    wide_x, wide_y = lax.axis_size("gx"), lax.axis_size("gy")
    count = wide_x * wide_y
    hbm = pl.BlockSpec(memory_space=pltpu.HBM)
    rounds = 2 * LAYERS
    result = pl.pallas_call(
        functools.partial(kernel, wide_x, wide_y, cells_x, cells_y),
        out_shape=jax.ShapeDtypeStruct((cells, chans, slots), BF),
        in_specs=[hbm] * 11,
        out_specs=hbm,
        scratch_shapes=[
            pltpu.VMEM((cells, chans, slots), BF),
            pltpu.SemaphoreType.DMA((HALVES, cells // 8)),
            pltpu.SMEM((cells_x, cells_y), jnp.int32),
            pltpu.SMEM((cells_x, cells_y, OFFSETS), jnp.int32),
            pltpu.VMEM((cells, chans, slots), BF),
            pltpu.VMEM((cells, rank, slots), BF),
            pltpu.VMEM((cells, rank, slots), BF),
            pltpu.VMEM((1, pairs), jnp.int32),
            pltpu.VMEM((1, pairs), jnp.int32),
            pltpu.VMEM((1, pairs), jnp.int32),
            pltpu.VMEM((pairs, rank * rank), BF),
            pltpu.VMEM((LAYERS, chans, chans), BF),
            pltpu.VMEM((cells, 4 * rank, slots), BF),
            pltpu.SemaphoreType.DMA((10,)),
            pltpu.VMEM((cells * OFFSETS, slots, slots), BF),
            pltpu.VMEM((count, LANES, LANES), BF),
            pltpu.VMEM((LAYERS, cells_x + 2, cells_y + 2, chans, slots), BF),
            pltpu.VMEM((HALVES, cells, ROWS, LANES), BF),
            pltpu.VMEM((rounds, count, ROWS, LANES), BF),
            pltpu.VMEM((rounds, count, ROWS, LANES), BF),
            pltpu.VMEM((count * ROWS + ROWS, LANES), F32),
            pltpu.VMEM((cells * ROWS + ROWS, LANES), F32),
            pltpu.VMEM((cells, 4 * rank, slots), BF),
            pltpu.VMEM((count, LANES), F32),
            pltpu.VMEM((count, LANES), F32),
            pltpu.VMEM((count, LANES), F32),
            pltpu.VMEM((count, LANES), F32),
            pltpu.VMEM((2 * cells, count), BF),
            pltpu.VMEM((2, 8, LANES), jnp.int32),
            pltpu.SMEM((2, 8, LANES), jnp.int32),
            pltpu.VMEM((cells, chans, slots), F32),
            pltpu.VMEM((cells, slots), F32),
            pltpu.SemaphoreType.DMA((4,)),
            pltpu.SemaphoreType.DMA,
            pltpu.SemaphoreType.DMA((rounds,)),
            pltpu.SemaphoreType.DMA((rounds,)),
            pltpu.SemaphoreType.DMA((3, 8)),
            pltpu.SemaphoreType.DMA((3, 8)),
            pltpu.SemaphoreType.DMA((4,)),
            pltpu.SemaphoreType.REGULAR,
        ],
        compiler_params=pltpu.CompilerParams(
            collective_id=0, has_side_effects=True, vmem_limit_bytes=56 << 20
        ),
    )(
        cell_count,
        near_mask,
        features.reshape(cells, chans, slots),
        near_tiles.reshape(cells * OFFSETS, slots, slots),
        projection_basis.reshape(cells, rank, slots),
        expand_basis.reshape(cells, rank, slots),
        far_source.reshape(1, pairs),
        far_owner.reshape(1, pairs),
        far_cell.reshape(1, pairs),
        distant_pair_matrix.reshape(pairs, rank * rank),
        mixing,
    )
    return result.reshape(cells_x, cells_y, chans, slots)


def solution(mesh):
    placed = (
        P("gx", "gy", None, None),
        P("gx", "gy"),
        P("gx", "gy", None),
        P("gx", "gy", None, None, None),
        P("gx", "gy", None, None),
        P("gx", "gy", None, None),
        P("gx", "gy", None),
        P("gx", "gy", None, None),
        P("gx", "gy", None),
        P("gx", "gy", None, None),
        P(),
    )
    return jax.shard_map(
        shards, mesh=mesh, in_specs=placed, out_specs=P("gx", "gy", None, None), check_vma=False
    )
```
